512 devices in a mesh: row: 32 (over x, y), col: 16 (over z, core).
Axes of the slice: x: 4, y: 8, z: 8, core: 2. Of those that a mesh axis runs over, the one named last changes fastest.
Arguments:
- momentum: float32 [8192, 13312], P('row', 'col'), may hold values from -200 to 200
- gradient: bfloat16 [8192, 13312], P('row', 'col'), may hold values from -6 to 6
- basis: float32 [13312, 256], P('col'), may hold values from -0.0546875 to 0.0546875
Outputs:
- new_momentum: float32 [8192, 13312], P('row', 'col')
- new_basis: float32 [13312, 256], P('col')
- update: bfloat16 [8192, 13312], P('row', 'col')
The draws below stay inside these ranges and needn't reach their ends.
All inputs are finite; a program needn't handle non-finite values.
Results may differ from the reference program's by a relative error of at most 0.001.
Values sent between devices are 32-bit elements; how exact they have to be, the bound alone decides.
A program may use at most 64 MiB of HBM per device.

```python
import math
import jax
import jax.numpy as jnp
from jax import lax

M = 8192
N = 13312
R = 256


def draw_momentum(key, part):
    key = jax.random.fold_in(key, 7)
    keys = jax.random.split(key, 3)
    row_pos = jnp.arange(M, dtype=jnp.float32) / M
    col_pos = jnp.arange(N, dtype=jnp.float32) / N
    col_scale = jnp.exp(jax.random.uniform(keys[2], (N,), jnp.float32, 0.0, math.log(10.0))) * (1.0 + 2.0 * col_pos)
    values = jnp.clip(jax.random.normal(keys[0], (M, N), jnp.float32), -6.0, 6.0)
    row_scale = jnp.exp(jax.random.uniform(keys[1], (M,), jnp.float32, 0.0, math.log(10.0)))
    row_scale = row_scale * (1.0 + 2.0 * row_pos)
    return values * row_scale[:, None] * col_scale[None, :] / 30.0


def steps_of(stream_key, shape, cuts, smallest, top_value):
    def one(dim, shards_of):
        draws = jax.random.uniform(jax.random.fold_in(jax.random.fold_in(stream_key, 6), dim), (shards_of,), jnp.float32, smallest / len(cuts), top_value / len(cuts))
        return jnp.repeat(jnp.exp(draws), shape[dim] // shards_of).reshape((-1,) + (1,) * (len(shape) - dim - 1))

    gain = one(*cuts[0])
    for cut in cuts[1:]:
        gain = gain * one(*cut)
    return gain


def centred(own_key, dims, width, most, shards=(), kind=jnp.bfloat16):
    entries = jax.random.normal(own_key, dims, jnp.float32) * width
    if len(shards) > 0:
        entries = steps_of(own_key, dims, shards, -0.22, 0.18) * entries
    return jnp.clip(entries, min=-most, max=most).astype(kind)


def setup_inputs(seed: int = 0) -> dict:
    key_of = jax.random.split(jax.random.key(seed), 4)
    momentum = draw_momentum(jax.random.fold_in(key_of[3], 71), 0)
    gradient = centred(key_of[1], (M, N), 1.0, 6.0, ((0, 32), (1, 16)))
    basis = centred(key_of[2], (N, R), N ** -0.5, 0.0546875, ((0, 16),), jnp.float32)
    return {"momentum": momentum, "gradient": gradient, "basis": basis}


KEEP_RATE = 0.95
NORM_EPS = 1e-06

def reference(momentum, gradient, basis):
    high = lax.Precision.HIGHEST
    buffer = momentum + gradient.astype(jnp.float32)
    power = jnp.dot(buffer.astype(jnp.float32), basis.astype(jnp.float32), precision=high, preferred_element_type=jnp.float32)
    gram = jnp.dot(power.T.astype(jnp.float32), power.astype(jnp.float32), precision=high, preferred_element_type=jnp.float32)
    lower = jnp.linalg.cholesky(gram)
    ortho = lax.linalg.triangular_solve(lower, power, left_side=False, lower=True, transpose_a=True)
    right = jnp.dot(buffer.T.astype(jnp.float32), ortho.astype(jnp.float32), precision=high, preferred_element_type=jnp.float32)
    norms = jnp.sqrt(lax.optimization_barrier(jnp.sum(right * right, axis=0))) + NORM_EPS
    new_basis = right / norms[None, :]
    new_momentum = buffer - (1.0 - KEEP_RATE) * jnp.dot(ortho.astype(jnp.float32), right.T.astype(jnp.float32), precision=high, preferred_element_type=jnp.float32)
    factor = math.sqrt(M * N / R)
    update = (factor * jnp.dot(ortho.astype(jnp.float32), new_basis.T.astype(jnp.float32), precision=high, preferred_element_type=jnp.float32)).astype(jnp.bfloat16)
    return (new_momentum, new_basis, update)
```

```python
import functools
import math

import jax
import jax.numpy as jnp
from jax import lax
from jax.experimental import pallas as pl
from jax.experimental.pallas import tpu as pltpu
from jax.sharding import PartitionSpec as P

M = 8192
N = 13312
R = 256
KEEP_RATE = 0.95
NORM_EPS = 1e-06

NX, NY, NZ = 4, 8, 8
ROWS = M // (NX * NY)
COLS = N // (2 * NZ)
WIDE = 896
CUT = 512
REST = WIDE - CUT
F32 = jnp.float32
BF16 = jnp.bfloat16
MESH = pl.DeviceIdType.MESH


def dot(a, b, dims):
    return lax.dot_general(
        a, b, (dims, ((), ())), precision=lax.Precision.HIGHEST, preferred_element_type=F32
    )


def factor_step(k, a, rs):
    off = pl.multiple_of(k * 8, 8)
    diag = pltpu.roll(a[pl.ds(off, 8), :R], lax.rem(R - off, R), 1)[:, :128]
    s = {}
    for j in range(8):
        col = jnp.broadcast_to(diag[:, j : j + 1], (8, 128))
        for i in range(j, 8):
            s[i, j] = jnp.broadcast_to(col[i : i + 1, :], (8, 128))
    rows = [a[pl.ds(off + i, 1), :] for i in range(8)]
    for j in range(8):
        d = lax.rsqrt(s[j, j])
        rows[j] = rows[j] * jnp.concatenate([d[:1]] * 4, axis=1)
        rs[j : j + 1, :] = rows[j]
        l = {i: s[i, j] * d for i in range(j + 1, 8)}
        for i in range(j + 1, 8):
            rows[i] = rows[i] - jnp.concatenate([l[i][:1]] * 4, axis=1) * rows[j]
            for c in range(j + 1, i + 1):
                s[i, c] = s[i, c] - l[i] * l[c]
    r = rs[...]
    a[pl.ds(off, 8), R:] = r[:, R:]
    hi = r.astype(BF16).astype(F32)
    mi = (r - hi).astype(BF16).astype(F32)
    lo = r - hi - mi
    lane = lax.broadcasted_iota(jnp.int32, (48, R), 1)
    lhs = jnp.concatenate([hi, hi, mi, mi, hi, lo], axis=0)[:, :R]
    lhs = jnp.where(lane >= off + 8, lhs, 0.0).astype(BF16)
    rhs = jnp.concatenate([hi, mi, hi, mi, lo, hi], axis=0).astype(BF16)
    a[...] = a[...] - lax.dot_general(
        lhs, rhs, (((0,), (0,)), ((), ())), preferred_element_type=F32
    )


def kernel(
    mom_ref, grad_ref, basis_ref,
    nm_ref, nb_ref, up_ref,
    buf, part, core_in, half, z_in, power,
    gram, gx, gy, gram_all,
    wt1, wt2, wx1_in, sx1, wy1_in, wy2_in, sy2, wx2_in, wf1, wf2,
    a, rs, right, sq,
    s_core, r_core, s_zr, r_zr, s_zg, r_zg, s_cg, r_cg,
    s_gx, r_gx, s_gy, r_gy, s_gz, r_gz, s_gc, r_gc,
    s_x1, r_x1, s_y1, r_y1, s_y2, r_y2, s_x2, r_x2,
    s_y1g, r_y1g, s_x1g, r_x1g, s_x2g, r_x2g, s_y2g, r_y2g,
    s_sq, r_sq,
):
    row = lax.axis_index("row")
    col = lax.axis_index("col")
    x, y = row // NY, lax.rem(row, NY)
    z, core = col // 2, lax.rem(col, 2)

    def x_peer(k):
        xt = lax.rem(x + k, NX)
        return xt, (xt * NY + y, col)

    def y_peer(k):
        yt = lax.rem(y + k, NY)
        return yt, (x * NY + yt, col)

    def z_peer(k):
        zt = lax.rem(z + k, NZ)
        return zt, (row, zt * 2 + core)

    sibling = (row, z * 2 + 1 - core)

    def col_peer(k):
        return (row, lax.rem(col + k, 2 * NZ))

    sent = []

    def send(src, dst, ssem, rsem, dev):
        copy = pltpu.make_async_remote_copy(
            src_ref=src, dst_ref=dst, send_sem=ssem, recv_sem=rsem,
            device_id=dev, device_id_type=MESH,
        )
        copy.start()
        sent.append(copy)
        return copy

    def rows8(start, n):
        return pl.ds(pl.multiple_of(start, 8), n)

    barrier = pltpu.get_barrier_semaphore()
    peers = [x_peer(k)[1] for k in range(1, NX)]
    peers += [y_peer(k)[1] for k in range(1, NY)]
    peers += [col_peer(k) for k in range(1, 2 * NZ)]
    for dev in peers:
        pl.semaphore_signal(barrier, inc=1, device_id=dev, device_id_type=MESH)

    buf[:, COLS:] = jnp.zeros((ROWS, WIDE - COLS), F32)
    buf[:, :COLS] = mom_ref[...] + grad_ref[...].astype(F32)
    part[...] = dot(buf[:, :COLS], basis_ref[...], ((1,), (0,)))

    pl.semaphore_wait(barrier, len(peers))

    c = send(part.at[rows8((1 - core) * 128, 128), :], core_in, s_core, r_core, sibling)
    c.wait_recv()
    half[...] = part[rows8(core * 128, 128), :] + core_in[...]
    cs = []
    for k in range(1, NZ):
        zt, dev = z_peer(k)
        cs.append(send(half.at[rows8(zt * 16, 16), :], z_in.at[k - 1], s_zr.at[k - 1], r_zr.at[k - 1], dev))
    total = half[rows8(z * 16, 16), :]
    for k in range(1, NZ):
        cs[k - 1].wait_recv()
        total = total + z_in[k - 1]

    def gather_col(ref, ss, rr, sc, rc):
        mine = ref.at[rows8(core * 128 + z * 16, 16), :]
        cs = []
        for k in range(1, NZ):
            cs.append(send(mine, mine, ss.at[k - 1], rr.at[k - 1], z_peer(k)[1]))
        fs = [send(mine, mine, sc.at[0], rc.at[0], sibling)]
        for k in range(1, NZ):
            cs[k - 1].wait_recv()
            zs = lax.rem(z + NZ - k, NZ)
            theirs = ref.at[rows8(core * 128 + zs * 16, 16), :]
            fs.append(send(theirs, theirs, sc.at[k], rc.at[k], sibling))
        return fs

    power[rows8(core * 128 + z * 16, 16), :] = total
    for c in gather_col(power, s_zg, r_zg, s_cg, r_cg):
        c.wait_recv()

    gram[...] = dot(power[...], power[...], ((0,), (0,)))
    gs = rows8(core * 128 + z * 16, 16)
    cs = []
    for k in range(1, NX):
        cs.append(send(gram.at[gs, :], gx.at[x], s_gx.at[k - 1], r_gx.at[k - 1], x_peer(k)[1]))
    gx[x] = gram[gs, :]

    wt1[...] = dot(power[...], buf[:, :CUT], ((0,), (0,)))
    c_x1 = []
    for k in range(1, NX):
        xt, dev = x_peer(k)
        c_x1.append(send(wt1.at[rows8(xt * 64, 64), :], wx1_in.at[k - 1], s_x1.at[k - 1], r_x1.at[k - 1], dev))

    for c in cs:
        c.wait_recv()
    gy[y] = (gx[0] + gx[1]) + (gx[2] + gx[3])
    cs = []
    for k in range(1, NY):
        cs.append(send(gy.at[y], gy.at[y], s_gy.at[k - 1], r_gy.at[k - 1], y_peer(k)[1]))

    wt2[...] = dot(power[...], buf[:, CUT:], ((0,), (0,)))
    c_y2 = []
    for k in range(1, NY):
        yt, dev = y_peer(k)
        c_y2.append(send(wt2.at[rows8(yt * 32, 32), :], wy2_in.at[k - 1], s_y2.at[k - 1], r_y2.at[k - 1], dev))

    for c in cs:
        c.wait_recv()
    gram_all[gs, :] = ((gy[0] + gy[1]) + (gy[2] + gy[3])) + ((gy[4] + gy[5]) + (gy[6] + gy[7]))
    fs = gather_col(gram_all, s_gz, r_gz, s_gc, r_gc)

    for c in c_x1:
        c.wait_recv()
    sx1[...] = (wt1[rows8(x * 64, 64), :] + wx1_in[0]) + (wx1_in[1] + wx1_in[2])
    c_y1 = []
    for k in range(1, NY):
        yt, dev = y_peer(k)
        c_y1.append(send(sx1.at[rows8(yt * 8, 8), :], wy1_in.at[k - 1], s_y1.at[k - 1], r_y1.at[k - 1], dev))

    for c in fs:
        c.wait_recv()
    a[:, :R] = gram_all[...]
    ii = lax.broadcasted_iota(jnp.int32, (R, R), 0)
    jj = lax.broadcasted_iota(jnp.int32, (R, R), 1)
    a[:, R:] = jnp.where(ii == jj, 1.0, 0.0).astype(F32)

    def factor(lo, hi):
        def body(k, carry):
            factor_step(k, a, rs)
            return carry
        lax.fori_loop(lo, hi, body, 0)

    for c in c_y2:
        c.wait_recv()
    acc = wt2[rows8(y * 32, 32), :]
    for k in range(NY - 1):
        acc = acc + wy2_in[k]
    sy2[...] = acc
    c_x2 = []
    for k in range(1, NX):
        xt, dev = x_peer(k)
        c_x2.append(send(sy2.at[rows8(xt * 8, 8), :], wx2_in.at[k - 1], s_x2.at[k - 1], r_x2.at[k - 1], dev))

    factor(0, 8)

    for c in c_y1:
        c.wait_recv()
    acc = sx1[rows8(y * 8, 8), :]
    for k in range(NY - 1):
        acc = acc + wy1_in[k]
    w1 = wf1.at[rows8(x * 64 + y * 8, 8), :]
    w1[...] = acc
    c_y1g = [send(w1, w1, s_y1g.at[k - 1], r_y1g.at[k - 1], y_peer(k)[1]) for k in range(1, NY)]
    for c in c_x2:
        c.wait_recv()
    w2 = wf2.at[rows8(y * 32 + x * 8, 8), :]
    w2[...] = (sy2[rows8(x * 8, 8), :] + wx2_in[0]) + (wx2_in[1] + wx2_in[2])
    c_x2g = [send(w2, w2, s_x2g.at[k - 1], r_x2g.at[k - 1], x_peer(k)[1]) for k in range(1, NX)]

    factor(8, 16)

    for c in c_x2g:
        c.wait_recv()
    w2 = wf2.at[rows8(y * 32, 32), :]
    c_y2g = [send(w2, w2, s_y2g.at[k - 1], r_y2g.at[k - 1], y_peer(k)[1]) for k in range(1, NY)]
    for c in c_y1g:
        c.wait_recv()
    w1 = wf1.at[rows8(x * 64, 64), :]
    c_x1g = [send(w1, w1, s_x1g.at[k - 1], r_x1g.at[k - 1], x_peer(k)[1]) for k in range(1, NX)]

    factor(16, 32)

    inv = a[:, R:]
    ortho = dot(power[...], inv, ((1,), (1,)))
    for c in c_y2g:
        c.wait_recv()
    for c in c_x1g:
        c.wait_recv()
    right[:, :CUT] = dot(inv, wf1[...], ((1,), (0,)))
    right[:, CUT:] = dot(inv, wf2[...], ((1,), (0,)))
    sq[col] = dot(jnp.ones((8, WIDE), F32), right[...] * right[...], ((1,), (1,)))
    cs = [send(sq.at[col], sq.at[col], s_sq.at[k - 1], r_sq.at[k - 1], col_peer(k)) for k in range(1, 2 * NZ)]

    nm_ref[...] = buf[:, :COLS] - (1.0 - KEEP_RATE) * dot(ortho, right[:, :COLS], ((1,), (0,)))

    for c in cs:
        c.wait_recv()
    squares = sq[0]
    for k in range(1, 2 * NZ):
        squares = squares + sq[k]
    norms = jnp.sqrt(squares[:1]) + NORM_EPS
    nb_ref[...] = right[...].T[:COLS] / norms
    up_ref[...] = (math.sqrt(M * N / R) * dot(ortho / norms, right[:, :COLS], ((1,), (0,)))).astype(BF16)

    for c in sent:
        c.wait_send()


def shards(momentum, gradient, basis):
    vmem = pl.BlockSpec(memory_space=pltpu.VMEM)
    v = lambda *s: pltpu.VMEM(s, F32)
    d = pltpu.SemaphoreType.DMA
    sems = []
    for n in (0, 7, 7, 8, 3, 7, 7, 8, 3, 7, 7, 3, 7, 3, 3, 7, 15):
        sems += [d(()) if n == 0 else d((n,))] * 2
    return pl.pallas_call(
        kernel,
        out_shape=(
            jax.ShapeDtypeStruct((ROWS, COLS), F32),
            jax.ShapeDtypeStruct((COLS, R), F32),
            jax.ShapeDtypeStruct((ROWS, COLS), BF16),
        ),
        in_specs=[vmem] * 3,
        out_specs=(vmem,) * 3,
        scratch_shapes=[
            v(ROWS, WIDE), v(ROWS, R), v(128, R), v(128, R), v(7, 16, R), v(ROWS, R),
            v(R, R), v(NX, 16, R), v(NY, 16, R), v(R, R),
            v(R, CUT), v(R, REST), v(3, 64, CUT), v(64, CUT), v(7, 8, CUT),
            v(7, 32, REST), v(32, REST), v(3, 8, REST), v(R, CUT), v(R, REST),
            v(R, 2 * R), v(8, 2 * R), v(R, WIDE), v(2 * NZ, 8, R),
            *sems,
        ],
        compiler_params=pltpu.CompilerParams(
            collective_id=0, has_side_effects=True, vmem_limit_bytes=48 << 20
        ),
    )(momentum, gradient, basis)


def solution(mesh):
    return jax.shard_map(
        shards,
        mesh=mesh,
        in_specs=(P("row", "col"), P("row", "col"), P("col", None)),
        out_specs=(P("row", "col"), P("col", None), P("row", "col")),
        check_vma=False,
    )
```

```python
import functools
import math

import jax
import jax.numpy as jnp
from jax import lax
from jax.experimental import pallas as pl
from jax.experimental.pallas import tpu as pltpu
from jax.sharding import PartitionSpec as P

M = 8192
N = 13312
R = 256
KEEP_RATE = 0.95
NORM_EPS = 1e-06

NX, NY, NZ = 4, 8, 8
ROWS = M // (NX * NY)
COLS = N // (2 * NZ)
CUT = 512
FIRST = CUT // NX
SMALL = FIRST // NY
SECOND = (COLS - CUT) // NY
F32 = jnp.float32
BF16 = jnp.bfloat16
MESH = pl.DeviceIdType.MESH


def dot(a, b, dims):
    return lax.dot_general(
        a, b, (dims, ((), ())), precision=lax.Precision.HIGHEST, preferred_element_type=F32
    )


def dot3(a, b, dims):
    ah = a.astype(BF16)
    bh = b.astype(BF16)
    al = (a - ah.astype(F32)).astype(BF16)
    bl = (b - bh.astype(F32)).astype(BF16)
    one = lambda p, q: lax.dot_general(p, q, (dims, ((), ())), preferred_element_type=F32)
    return one(ah, bh) + (one(ah, bl) + one(al, bh))


def factor_step(k, a, rs):
    off = pl.multiple_of(k * 8, 8)
    diag = pltpu.roll(a[pl.ds(off, 8), :R], lax.rem(R - off, R), 1)[:, :128]
    s = {}
    for j in range(8):
        col = jnp.broadcast_to(diag[:, j : j + 1], (8, 128))
        for i in range(j, 8):
            s[i, j] = jnp.broadcast_to(col[i : i + 1, :], (8, 128))
    rows = [a[pl.ds(off + i, 1), :] for i in range(8)]
    for j in range(8):
        d = lax.rsqrt(s[j, j])
        rows[j] = rows[j] * jnp.concatenate([d[:1]] * 4, axis=1)
        rs[j : j + 1, :] = rows[j]
        l = {i: s[i, j] * d for i in range(j + 1, 8)}
        for i in range(j + 1, 8):
            rows[i] = rows[i] - jnp.concatenate([l[i][:1]] * 4, axis=1) * rows[j]
            for c in range(j + 1, i + 1):
                s[i, c] = s[i, c] - l[i] * l[c]
    r = rs[...]
    a[pl.ds(off, 8), R:] = r[:, R:]
    hi = r.astype(BF16).astype(F32)
    mi = (r - hi).astype(BF16).astype(F32)
    lo = r - hi - mi
    lane = lax.broadcasted_iota(jnp.int32, (48, R), 1)
    lhs = jnp.concatenate([hi, hi, mi, mi, hi, lo], axis=0)[:, :R]
    lhs = jnp.where(lane >= off + 8, lhs, 0.0).astype(BF16)
    rhs = jnp.concatenate([hi, mi, hi, mi, lo, hi], axis=0).astype(BF16)
    a[...] = a[...] - lax.dot_general(
        lhs, rhs, (((0,), (0,)), ((), ())), preferred_element_type=F32
    )


def kernel(
    mom_hbm, grad_hbm, basis_hbm,
    nm_ref, right_ref, ortho_ref, norms_ref,
    mom_ref, grad_ref, basis_ref, buf, part, core_in, half, z_in, power,
    gram, gx, gy, gram_all,
    wt, wx1_in, sx1, wy1_in, wy2_in, sy2, wx2_in, wx3_in, wf,
    a, rs, sq,
    s_core, r_core, s_zr, r_zr, s_zg, r_zg, s_cg, r_cg,
    s_gx, r_gx, s_gy, r_gy, s_gz, r_gz, s_gc, r_gc,
    s_x1, r_x1, s_y1, r_y1, s_y2, r_y2, s_x2, r_x2, s_x3, r_x3,
    s_y1g, r_y1g, s_x1g, r_x1g, s_x2g, r_x2g, s_y2g, r_y2g,
    s_sq, r_sq, s_in,
):
    loads = [
        pltpu.make_async_copy(src, dst, s_in.at[i])
        for i, (src, dst) in enumerate(((mom_hbm, mom_ref), (grad_hbm, grad_ref), (basis_hbm, basis_ref)))
    ]
    for load in loads:
        load.start()
    row = lax.axis_index("row")
    col = lax.axis_index("col")
    x, y = row // NY, lax.rem(row, NY)
    z, core = col // 2, lax.rem(col, 2)

    def x_peer(k):
        xt = lax.rem(x + k, NX)
        return xt, (xt * NY + y, col)

    def y_peer(k):
        yt = lax.rem(y + k, NY)
        return yt, (x * NY + yt, col)

    def z_peer(k):
        zt = lax.rem(z + k, NZ)
        return zt, (row, zt * 2 + core)

    sibling = (row, z * 2 + 1 - core)

    def col_peer(k):
        return (row, lax.rem(col + k, 2 * NZ))

    sent = []

    def send(src, dst, ssem, rsem, dev):
        copy = pltpu.make_async_remote_copy(
            src_ref=src, dst_ref=dst, send_sem=ssem, recv_sem=rsem,
            device_id=dev, device_id_type=MESH,
        )
        copy.start()
        sent.append(copy)
        return copy

    def rows8(start, n):
        return pl.ds(pl.multiple_of(start, 8), n)

    barrier = pltpu.get_barrier_semaphore()
    peers = [x_peer(k)[1] for k in range(1, NX)]
    peers += [y_peer(k)[1] for k in range(1, NY)]
    peers += [col_peer(k) for k in range(1, 2 * NZ)]
    for dev in peers:
        pl.semaphore_signal(barrier, inc=1, device_id=dev, device_id_type=MESH)

    with jax.named_scope("partial_power"):
        for load in loads:
            load.wait()
        buf[...] = mom_ref[...] + grad_ref[...].astype(F32)
        part[...] = dot(buf[...], basis_ref[...], ((0,), (0,)))

    with jax.named_scope("entry"):
        pl.semaphore_wait(barrier, len(peers))

    with jax.named_scope("power_core"):
        c = send(part.at[rows8((1 - core) * 128, 128), :], core_in, s_core, r_core, sibling)
        c.wait_recv()
        half[...] = part[rows8(core * 128, 128), :] + core_in[...]
    with jax.named_scope("power_z"):
        cs = []
        for k in range(1, NZ):
            zt, dev = z_peer(k)
            cs.append(send(half.at[rows8(zt * 16, 16), :], z_in.at[k - 1], s_zr.at[k - 1], r_zr.at[k - 1], dev))
        total = half[rows8(z * 16, 16), :]
        for k in range(1, NZ):
            cs[k - 1].wait_recv()
            total = total + z_in[k - 1]

    mine16 = rows8(core * 128 + z * 16, 16)

    def gather_col(ref, ss, rr, sc, rc):
        mine = ref.at[mine16, :]
        cs = []
        for k in range(1, NZ):
            cs.append(send(mine, mine, ss.at[k - 1], rr.at[k - 1], z_peer(k)[1]))
        fs = [send(mine, mine, sc.at[0], rc.at[0], sibling)]
        for k in range(1, NZ):
            cs[k - 1].wait_recv()
            zs = lax.rem(z + NZ - k, NZ)
            theirs = ref.at[rows8(core * 128 + zs * 16, 16), :]
            fs.append(send(theirs, theirs, sc.at[k], rc.at[k], sibling))
        return fs

    with jax.named_scope("power_gather"):
        power[mine16, :] = total
        for c in gather_col(power, s_zg, r_zg, s_cg, r_cg):
            c.wait_recv()

    with jax.named_scope("gram_dot"):
        gram[...] = dot(power[...], power[...], ((0,), (0,)))
        cs = []
        for k in range(1, NX):
            cs.append(send(gram.at[mine16, :], gx.at[x], s_gx.at[k - 1], r_gx.at[k - 1], x_peer(k)[1]))
        gx[x] = gram[mine16, :]

    with jax.named_scope("w_dot_first"):
        wt[:CUT] = dot(buf[:CUT], power[...], ((1,), (0,)))
        c_x1 = []
        for k in range(1, NX):
            xt, dev = x_peer(k)
            c_x1.append(send(wt.at[rows8(xt * FIRST, FIRST), :], wx1_in.at[k - 1], s_x1.at[k - 1], r_x1.at[k - 1], dev))

    with jax.named_scope("gram_x"):
        for c in cs:
            c.wait_recv()
        gy[y] = (gx[0] + gx[1]) + (gx[2] + gx[3])
        cs = []
        for k in range(1, NY):
            cs.append(send(gy.at[y], gy.at[y], s_gy.at[k - 1], r_gy.at[k - 1], y_peer(k)[1]))

    with jax.named_scope("w_dot_second"):
        wt[CUT:] = dot(buf[CUT:], power[...], ((1,), (0,)))
        c_y2 = []
        for k in range(1, NY):
            yt, dev = y_peer(k)
            c_y2.append(send(wt.at[rows8(CUT + yt * SECOND, SECOND), :], wy2_in.at[k - 1], s_y2.at[k - 1], r_y2.at[k - 1], dev))

    with jax.named_scope("gram_y"):
        for c in cs:
            c.wait_recv()
        gram_all[mine16, :] = ((gy[0] + gy[1]) + (gy[2] + gy[3])) + ((gy[4] + gy[5]) + (gy[6] + gy[7]))
    with jax.named_scope("gram_gather"):
        fs = gather_col(gram_all, s_gz, r_gz, s_gc, r_gc)

    with jax.named_scope("w1_x"):
        for c in c_x1:
            c.wait_recv()
        sx1[...] = (wt[rows8(x * FIRST, FIRST), :] + wx1_in[0]) + (wx1_in[1] + wx1_in[2])
        c_y1 = []
        for k in range(1, NY):
            yt, dev = y_peer(k)
            c_y1.append(send(sx1.at[rows8(yt * SMALL, SMALL), :], wy1_in.at[k - 1], s_y1.at[k - 1], r_y1.at[k - 1], dev))

    with jax.named_scope("gram_wait"):
        for c in fs:
            c.wait_recv()
        a[:, :R] = gram_all[...]
        ii = lax.broadcasted_iota(jnp.int32, (R, R), 0)
        jj = lax.broadcasted_iota(jnp.int32, (R, R), 1)
        a[:, R:] = jnp.where(ii == jj, 1.0, 0.0).astype(F32)

    def factor(lo, hi):
        def body(k, carry):
            factor_step(k, a, rs)
            return carry
        lax.fori_loop(lo, hi, body, 0)

    with jax.named_scope("factor_0"):
        factor(0, 4)

    with jax.named_scope("w2_y"):
        for c in c_y2:
            c.wait_recv()
        acc = wt[rows8(CUT + y * SECOND, SECOND), :]
        for k in range(NY - 1):
            acc = acc + wy2_in[k]
        sy2[...] = acc
        c_x2 = []
        wx3_in[x] = acc[32:]
        for k in range(1, NX):
            xt, dev = x_peer(k)
            c_x2.append(send(sy2.at[rows8(xt * 8, 8), :], wx2_in.at[k - 1], s_x2.at[k - 1], r_x2.at[k - 1], dev))
            c_x2.append(send(sy2.at[pl.ds(32, 8), :], wx3_in.at[x], s_x3.at[k - 1], r_x3.at[k - 1], dev))

    with jax.named_scope("factor_1"):
        factor(4, 12)

    with jax.named_scope("w1_y"):
        for c in c_y1:
            c.wait_recv()
        acc = sx1[rows8(y * SMALL, SMALL), :]
        for k in range(NY - 1):
            acc = acc + wy1_in[k]
        w1 = wf.at[rows8(x * FIRST + y * SMALL, SMALL), :]
        w1[...] = acc
        c_y1g = [send(w1, w1, s_y1g.at[k - 1], r_y1g.at[k - 1], y_peer(k)[1]) for k in range(1, NY)]
    with jax.named_scope("w2_x"):
        for c in c_x2:
            c.wait_recv()
        w2 = wf.at[rows8(CUT + y * SECOND + x * 8, 8), :]
        w2[...] = (sy2[rows8(x * 8, 8), :] + wx2_in[0]) + (wx2_in[1] + wx2_in[2])
        c_x2g = [send(w2, w2, s_x2g.at[k - 1], r_x2g.at[k - 1], x_peer(k)[1]) for k in range(1, NX)]
        wf[rows8(CUT + y * SECOND + 32, 8), :] = (wx3_in[0] + wx3_in[1]) + (wx3_in[2] + wx3_in[3])

    with jax.named_scope("factor_2"):
        factor(12, 20)

    with jax.named_scope("w2_x_gather"):
        for c in c_x2g:
            c.wait_recv()
        w2 = wf.at[rows8(CUT + y * SECOND, SECOND), :]
        c_y2g = [send(w2, w2, s_y2g.at[k - 1], r_y2g.at[k - 1], y_peer(k)[1]) for k in range(1, NY)]
    with jax.named_scope("w1_y_gather"):
        for c in c_y1g:
            c.wait_recv()
        w1 = wf.at[rows8(x * FIRST, FIRST), :]
        c_x1g = [send(w1, w1, s_x1g.at[k - 1], r_x1g.at[k - 1], x_peer(k)[1]) for k in range(1, NX)]

    with jax.named_scope("factor_3"):
        factor(20, 32)

    with jax.named_scope("ortho"):
        inv = a[:, R:]
        ortho_ref[...] = dot(power[...], inv, ((1,), (1,)))
    with jax.named_scope("w_gather"):
        for c in c_y2g:
            c.wait_recv()
        for c in c_x1g:
            c.wait_recv()
    with jax.named_scope("right"):
        right_ref[...] = dot(wf[...], inv, ((1,), (1,)))
    with jax.named_scope("squares"):
        rt = right_ref[...]
        sums = jnp.sum((rt * rt).reshape(COLS // 8, 8, R), axis=0)
        sq[col] = jnp.sum(sums, axis=0, keepdims=True)
        cs = [send(sq.at[col], sq.at[col], s_sq.at[k - 1], r_sq.at[k - 1], col_peer(k)) for k in range(1, 2 * NZ)]

    with jax.named_scope("momentum"):
        nm_ref[...] = buf[...] - (1.0 - KEEP_RATE) * dot3(right_ref[...], ortho_ref[...], ((1,), (1,)))

    with jax.named_scope("norms"):
        for c in cs:
            c.wait_recv()
        squares = sq[0]
        for k in range(1, 2 * NZ):
            squares = squares + sq[k]
        norms_ref[...] = jnp.broadcast_to(jnp.sqrt(squares) + NORM_EPS, (8, R))

    with jax.named_scope("wait_sent"):
        for c in sent:
            c.wait_send()


def finish(nm_ref, right_ref, ortho_ref, norms_ref, nm_out, nb_out, up_out, nb, up, sems):
    c_nm = pltpu.make_async_copy(nm_ref, nm_out, sems.at[0])
    c_nm.start()
    nb[...] = right_ref[...] / norms_ref[:1]
    c_nb = pltpu.make_async_copy(nb, nb_out, sems.at[1])
    c_nb.start()
    up[...] = (math.sqrt(M * N / R) * dot3(nb[...], ortho_ref[...], ((1,), (1,)))).astype(BF16)
    c_up = pltpu.make_async_copy(up, up_out, sems.at[2])
    c_up.start()
    c_nm.wait()
    c_nb.wait()
    c_up.wait()


def shards(momentum, gradient, basis):
    vmem = pl.BlockSpec(memory_space=pltpu.VMEM)
    hbm = pl.BlockSpec(memory_space=pltpu.HBM)
    v = lambda *s: pltpu.VMEM(s, F32)
    d = pltpu.SemaphoreType.DMA
    sems = []
    for n in (0, 7, 7, 8, 3, 7, 7, 8, 3, 7, 7, 3, 3, 7, 3, 3, 7, 15):
        sems += [d(()) if n == 0 else d((n,))] * 2
    out = jax.ShapeDtypeStruct
    nm, right, ortho, norms = pl.pallas_call(
        kernel,
        out_shape=(out((COLS, ROWS), F32), out((COLS, R), F32), out((ROWS, R), F32), out((8, R), F32)),
        in_specs=[hbm] * 3,
        out_specs=(vmem,) * 4,
        scratch_shapes=[
            v(COLS, ROWS), pltpu.VMEM((COLS, ROWS), BF16), v(COLS, R),
            v(COLS, ROWS), v(ROWS, R), v(128, R), v(128, R), v(7, 16, R), v(ROWS, R),
            v(R, R), v(NX, 16, R), v(NY, 16, R), v(R, R),
            v(COLS, R), v(3, FIRST, R), v(FIRST, R), v(7, SMALL, R), v(7, SECOND, R), v(SECOND, R),
            v(3, 8, R), v(NX, 8, R), v(COLS, R),
            v(R, 2 * R), v(8, 2 * R), v(2 * NZ, 1, R),
            *sems, d((3,)),
        ],
        compiler_params=pltpu.CompilerParams(
            collective_id=0, has_side_effects=True, vmem_limit_bytes=40 << 20
        ),
    )(momentum.T, gradient.T, basis)
    nm, nb, up = pl.pallas_call(
        finish,
        out_shape=(out((COLS, ROWS), F32), out((COLS, R), F32), out((COLS, ROWS), BF16)),
        in_specs=[vmem] * 4,
        out_specs=(hbm,) * 3,
        scratch_shapes=[v(COLS, R), pltpu.VMEM((COLS, ROWS), BF16), d((3,))],
        compiler_params=pltpu.CompilerParams(vmem_limit_bytes=16 << 20),
    )(nm, right, ortho, norms)
    return nm.T, nb, up.T


def solution(mesh):
    return jax.shard_map(
        shards,
        mesh=mesh,
        in_specs=(P("row", "col"), P("row", "col"), P("col", None)),
        out_specs=(P("row", "col"), P("col", None), P("row", "col")),
        check_vma=False,
    )
```

```python
import functools
import math

import jax
import jax.numpy as jnp
from jax import lax
from jax.experimental import pallas as pl
from jax.experimental.pallas import tpu as pltpu
from jax.sharding import PartitionSpec as P

M = 8192
N = 13312
R = 256
KEEP_RATE = 0.95
NORM_EPS = 1e-06

NX, NY, NZ = 4, 8, 8
ROWS = M // (NX * NY)
COLS = N // (2 * NZ)
CUT = 512
FIRST = CUT // NX
SMALL = FIRST // NY
SECOND = (COLS - CUT) // NY
PANEL = 32
FAR = (4, 3, 5, 2, 6, 1, 7)
NEAR = (1, 7, 2, 6, 3, 5, 4)
FAR_X = (2, 1, 3)
F32 = jnp.float32
BF16 = jnp.bfloat16
MESH = pl.DeviceIdType.MESH


def dot(a, b, dims):
    return lax.dot_general(
        a, b, (dims, ((), ())), precision=lax.Precision.HIGHEST, preferred_element_type=F32
    )


def dot3(a, b, dims):
    ah = a.astype(BF16)
    bh = b.astype(BF16)
    al = (a - ah.astype(F32)).astype(BF16)
    bl = (b - bh.astype(F32)).astype(BF16)
    one = lambda p, q: lax.dot_general(p, q, (dims, ((), ())), preferred_element_type=F32)
    return one(ah, bh) + (one(ah, bl) + one(al, bh))


def factor_panel(k, a):
    off = pl.multiple_of(k * PANEL, PANEL)
    base = pl.multiple_of(off // 128 * 128, 128)
    tiles = PANEL // 8
    sub = lax.broadcasted_iota(jnp.int32, (8, 128), 0)
    t = []
    for i in range(tiles):
        r = pl.ds(pl.multiple_of(off + 8 * i, 8), 8)
        row = a[r, :]
        own = pltpu.roll(a[r, pl.ds(base, 128)], lax.rem(128 - (off - base), 128), 1)
        t.append([own] + [row[:, 128 * q : 128 * q + 128] for q in range(4)])
    for b in range(tiles):
        cols = {}
        for i in range(b, tiles):
            for j in range(8):
                cols[i, j] = jnp.broadcast_to(t[i][0][:, 8 * b + j : 8 * b + j + 1], (8, 128))
        s = {}
        for j in range(8):
            for i in range(j, 8):
                s[i, j] = jnp.broadcast_to(cols[b, j][i : i + 1, :], (8, 128))
        scale = None
        for j in range(8):
            d = lax.rsqrt(s[j, j])
            l = {i: s[i, j] * d for i in range(j + 1, 8)}
            for m in range(j + 1, 8):
                for i in range(m, 8):
                    s[i, m] = s[i, m] - l[i] * l[m]
            pivot = [jnp.broadcast_to(t[b][q][j : j + 1, :], (8, 128)) * d for q in range(5)]
            for i in range(b, tiles):
                cols[i, j] = cols[i, j] * d
                for m in range(j + 1, 8):
                    cols[i, m] = cols[i, m] - cols[i, j] * l[m]
                times = cols[i, j] if i > b else jnp.where(sub > j, cols[i, j], 0.0)
                for q in range(5):
                    t[i][q] = t[i][q] - times * pivot[q]
            scale = d if j == 0 else jnp.where(sub == j, d, scale)
        for q in range(1, 5):
            t[b][q] = t[b][q] * scale
    r = jnp.concatenate([jnp.concatenate(t[i][1:], axis=1) for i in range(tiles)], axis=0)
    a[pl.ds(off, PANEL), R:] = r[:, R:]
    hi = r.astype(BF16).astype(F32)
    mi = (r - hi).astype(BF16).astype(F32)
    lo = r - hi - mi
    below = lax.broadcasted_iota(jnp.int32, (PANEL, R), 1) >= off + PANEL
    hl, ml, ll = (jnp.where(below, v[:, :R], 0.0).astype(BF16) for v in (hi, mi, lo))
    hr, mr, lr = hi.astype(BF16), mi.astype(BF16), lo.astype(BF16)
    lhs = jnp.concatenate([hl, hl, ml, ml, hl, ll], axis=0)
    rhs = jnp.concatenate([hr, mr, hr, mr, lr, hr], axis=0)
    a[...] = a[...] - lax.dot_general(
        lhs, rhs, (((0,), (0,)), ((), ())), preferred_element_type=F32
    )


def kernel(
    mom_hbm, grad_hbm, basis_hbm,
    nm_hbm, right_hbm, ortho_hbm, norms_hbm,
    nm_ref, right_ref, ortho_ref, norms_ref, mom_ref, grad_ref, basis_ref, buf, part, core_in, half, z_in, power,
    gram, gx, gy, gram_all,
    wt, wx1_in, sx1, wy1_in, wy2_in, sy2, wx2_in, wx3_in, wf,
    a, sq,
    s_core, r_core, s_zr, r_zr, s_zg, r_zg, s_cg, r_cg,
    s_gx, r_gx, s_gy, r_gy, s_gz, r_gz, s_gc, r_gc,
    s_x1, r_x1, s_y1, r_y1, s_y2, r_y2, s_x2, r_x2, s_x3, r_x3,
    s_y1g, r_y1g, s_x1g, r_x1g, s_x2g, r_x2g, s_y2g, r_y2g,
    s_sq, r_sq, s_in, s_out,
):
    loads = [
        pltpu.make_async_copy(src, dst, s_in.at[i])
        for i, (src, dst) in enumerate(((mom_hbm, mom_ref), (grad_hbm, grad_ref), (basis_hbm, basis_ref)))
    ]
    for load in loads:
        load.start()
    row = lax.axis_index("row")
    col = lax.axis_index("col")
    x, y = row // NY, lax.rem(row, NY)
    z, core = col // 2, lax.rem(col, 2)

    def x_peer(k):
        xt = lax.rem(x + k, NX)
        return xt, (xt * NY + y, col)

    def y_peer(k):
        yt = lax.rem(y + k, NY)
        return yt, (x * NY + yt, col)

    def z_peer(k):
        zt = lax.rem(z + k, NZ)
        return zt, (row, zt * 2 + core)

    sibling = (row, z * 2 + 1 - core)

    def col_peer(k):
        return (row, lax.rem(col + k, 2 * NZ))

    sent = []

    def send(src, dst, ssem, rsem, dev):
        copy = pltpu.make_async_remote_copy(
            src_ref=src, dst_ref=dst, send_sem=ssem, recv_sem=rsem,
            device_id=dev, device_id_type=MESH,
        )
        copy.start()
        sent.append(copy)
        return copy

    def rows8(start, n):
        return pl.ds(pl.multiple_of(start, 8), n)

    barrier = pltpu.get_barrier_semaphore()
    peers = [x_peer(k)[1] for k in range(1, NX)]
    peers += [y_peer(k)[1] for k in range(1, NY)]
    peers += [col_peer(k) for k in range(1, 2 * NZ)]
    for dev in peers:
        pl.semaphore_signal(barrier, inc=1, device_id=dev, device_id_type=MESH)

    ii = lax.broadcasted_iota(jnp.int32, (R, R), 0)
    jj = lax.broadcasted_iota(jnp.int32, (R, R), 1)
    a[:, R:] = jnp.where(ii == jj, 1.0, 0.0).astype(F32)

    mine128 = rows8(core * 128, 128)
    theirs128 = rows8((1 - core) * 128, 128)
    mine16 = rows8(core * 128 + z * 16, 16)

    def part_power(half_core):
        lanes = pl.ds(pl.multiple_of(half_core * 128, 128), 128)
        return dot(buf[:, lanes], basis_ref[...], ((0,), (0,)))

    def send_all(order, peer, src, dst, ss, rr):
        out = {}
        for k in order:
            at, dev = peer(k)
            out[k] = send(src(at), dst(k), ss.at[k - 1], rr.at[k - 1], dev)
        return out

    with jax.named_scope("partial_power"):
        for load in loads:
            load.wait()
        buf[...] = mom_ref[...] + grad_ref[...].astype(F32)
        part[theirs128, :] = part_power(1 - core)
        pl.semaphore_wait(barrier, len(peers))
        c = send(part.at[theirs128, :], core_in, s_core, r_core, sibling)
        part[mine128, :] = part_power(core)

    with jax.named_scope("power_sum"):
        c.wait_recv()
        half[...] = part[mine128, :] + core_in[...]
        cs = send_all(FAR, z_peer, lambda zt: half.at[rows8(zt * 16, 16), :], lambda k: z_in.at[k - 1], s_zr, r_zr)
        total = half[rows8(z * 16, 16), :]
        for k in NEAR:
            cs[k].wait_recv()
            total = total + z_in[k - 1]

    def gather_z(ref, ss, rr, sc, rc):
        mine = ref.at[mine16, :]
        cs = send_all(FAR, z_peer, lambda zt: mine, lambda k: mine, ss, rr)
        return cs, [send(mine, mine, sc.at[0], rc.at[0], sibling)]

    def gather_core(ref, cs, fs, sc, rc):
        for k in NEAR:
            cs[k].wait_recv()
            zs = lax.rem(z + NZ - k, NZ)
            theirs = ref.at[rows8(core * 128 + zs * 16, 16), :]
            fs.append(send(theirs, theirs, sc.at[k], rc.at[k], sibling))

    with jax.named_scope("power_gather"):
        power[mine16, :] = total
        cs, fs = gather_z(power, s_zg, r_zg, s_cg, r_cg)
        gather_core(power, cs, fs, s_cg, r_cg)
        for c in fs:
            c.wait_recv()

    with jax.named_scope("gram_dot"):
        gram[...] = dot(power[...], power[...], ((0,), (0,)))
        gx[x] = gram[mine16, :]
        c_gx = send_all(FAR_X, x_peer, lambda xt: gx.at[x], lambda k: gx.at[x], s_gx, r_gx)

    with jax.named_scope("w_dot"):
        wt[:CUT] = dot(buf[:CUT], power[...], ((1,), (0,)))
        c_x1 = send_all(FAR_X, x_peer, lambda xt: wt.at[rows8(xt * FIRST, FIRST), :], lambda k: wx1_in.at[k - 1], s_x1, r_x1)
        wt[CUT:] = dot(buf[CUT:], power[...], ((1,), (0,)))

    with jax.named_scope("gram_x"):
        for c in c_gx.values():
            c.wait_recv()
        gy[y] = (gx[0] + gx[1]) + (gx[2] + gx[3])
        c_gy = send_all(FAR, y_peer, lambda yt: gy.at[y], lambda k: gy.at[y], s_gy, r_gy)
        c_y2 = send_all(
            FAR, y_peer, lambda yt: wt.at[rows8(CUT + yt * SECOND, SECOND), :], lambda k: wy2_in.at[k - 1], s_y2, r_y2
        )

    with jax.named_scope("gram_y"):
        for c in c_gy.values():
            c.wait_recv()
        gram_all[mine16, :] = ((gy[0] + gy[1]) + (gy[2] + gy[3])) + ((gy[4] + gy[5]) + (gy[6] + gy[7]))
        c_gz, fs = gather_z(gram_all, s_gz, r_gz, s_gc, r_gc)

    with jax.named_scope("w1_x"):
        for c in c_x1.values():
            c.wait_recv()
        sx1[...] = (wt[rows8(x * FIRST, FIRST), :] + wx1_in[0]) + (wx1_in[1] + wx1_in[2])
        c_y1 = send_all(FAR, y_peer, lambda yt: sx1.at[rows8(yt * SMALL, SMALL), :], lambda k: wy1_in.at[k - 1], s_y1, r_y1)

    with jax.named_scope("w2_y"):
        for c in c_y2.values():
            c.wait_recv()
        acc = wt[rows8(CUT + y * SECOND, SECOND), :]
        for k in range(NY - 1):
            acc = acc + wy2_in[k]
        sy2[...] = acc
        wx3_in[x] = acc[32:]
        c_x2 = send_all(FAR_X, x_peer, lambda xt: sy2.at[rows8(xt * 8, 8), :], lambda k: wx2_in.at[k - 1], s_x2, r_x2)
        c_x3 = send_all(FAR_X, x_peer, lambda xt: sy2.at[pl.ds(32, 8), :], lambda k: wx3_in.at[x], s_x3, r_x3)

    with jax.named_scope("gram_z"):
        gather_core(gram_all, c_gz, fs, s_gc, r_gc)

    with jax.named_scope("w2_x"):
        for c in (*c_x2.values(), *c_x3.values()):
            c.wait_recv()
        w2 = wf.at[rows8(CUT + y * SECOND + x * 8, 8), :]
        w2[...] = (sy2[rows8(x * 8, 8), :] + wx2_in[0]) + (wx2_in[1] + wx2_in[2])
        c_x2g = send_all(FAR_X, x_peer, lambda xt: w2, lambda k: w2, s_x2g, r_x2g)
        wf[rows8(CUT + y * SECOND + 32, 8), :] = (wx3_in[0] + wx3_in[1]) + (wx3_in[2] + wx3_in[3])
    with jax.named_scope("w1_y"):
        for c in c_y1.values():
            c.wait_recv()
        acc = sx1[rows8(y * SMALL, SMALL), :]
        for k in range(NY - 1):
            acc = acc + wy1_in[k]
        w1 = wf.at[rows8(x * FIRST + y * SMALL, SMALL), :]
        w1[...] = acc
        c_y1g = send_all(FAR, y_peer, lambda yt: w1, lambda k: w1, s_y1g, r_y1g)

    def factor(lo, hi):
        def body(k, carry):
            factor_panel(k, a)
            return carry
        lax.fori_loop(lo, hi, body, 0)

    with jax.named_scope("factor_0"):
        for c in fs:
            c.wait_recv()
        a[:, :R] = gram_all[...]
        factor(0, 1)

    with jax.named_scope("w2_x_gather"):
        for c in c_x2g.values():
            c.wait_recv()
        w2y = wf.at[rows8(CUT + y * SECOND, SECOND), :]
        c_y2g = send_all(FAR, y_peer, lambda yt: w2y, lambda k: w2y, s_y2g, r_y2g)
    with jax.named_scope("factor_1"):
        factor(1, 2)
    with jax.named_scope("w1_y_gather"):
        for c in c_y1g.values():
            c.wait_recv()
        w1x = wf.at[rows8(x * FIRST, FIRST), :]
        c_x1g = send_all(FAR_X, x_peer, lambda xt: w1x, lambda k: w1x, s_x1g, r_x1g)

    with jax.named_scope("factor_2"):
        factor(2, R // PANEL)

    def store(src, dst, i):
        copy = pltpu.make_async_copy(src, dst, s_out.at[i])
        copy.start()
        return copy

    with jax.named_scope("ortho"):
        ortho_ref[...] = dot3(power[...], a[:, R:], ((1,), (1,)))
        stores = [store(ortho_ref, ortho_hbm, 1)]
    with jax.named_scope("right"):
        for c in c_x1g.values():
            c.wait_recv()
        right_ref[:CUT] = dot3(wf[:CUT], a[:, R:], ((1,), (1,)))
        for c in c_y2g.values():
            c.wait_recv()
        right_ref[CUT:] = dot3(wf[CUT:], a[:, R:], ((1,), (1,)))
    with jax.named_scope("squares"):
        rt = right_ref[...]
        sums = jnp.sum((rt * rt).reshape(COLS // 8, 8, R), axis=0)
        sq[col] = jnp.sum(sums, axis=0, keepdims=True)
        cs = [
            send(sq.at[col], sq.at[col], s_sq.at[k - 1], r_sq.at[k - 1], col_peer(k))
            for k in (8, 7, 9, 6, 10, 5, 11, 4, 12, 3, 13, 2, 14, 1, 15)
        ]
        stores.append(store(right_ref, right_hbm, 0))

    with jax.named_scope("momentum"):
        nm_ref[...] = buf[...] - (1.0 - KEEP_RATE) * dot3(right_ref[...], ortho_ref[...], ((1,), (1,)))
        stores.append(store(nm_ref, nm_hbm, 2))

    with jax.named_scope("norms"):
        for c in cs:
            c.wait_recv()
        squares = sq[0]
        for k in range(1, 2 * NZ):
            squares = squares + sq[k]
        norms_ref[...] = jnp.broadcast_to(jnp.sqrt(squares) + NORM_EPS, (8, R))
        stores.append(store(norms_ref, norms_hbm, 3))

    with jax.named_scope("wait_sent"):
        for c in stores:
            c.wait()
        for c in sent:
            c.wait_send()


def finish(nm_in, right_in, ortho_in, norms_in, nm_out, nb_out, up_out, nm, right, ortho, norms, nb, up, sems):
    def copy(i, src, dst):
        c = pltpu.make_async_copy(src, dst, sems.at[i])
        c.start()
        return c

    c_norms = copy(0, norms_in, norms)
    c_right = copy(1, right_in, right)
    c_ortho = copy(2, ortho_in, ortho)
    c_nm = copy(3, nm_in, nm)
    c_norms.wait()
    c_right.wait()
    nb[...] = right[...] / norms[:1]
    out = [copy(4, nb, nb_out)]
    c_nm.wait()
    out.append(copy(5, nm, nm_out))
    c_ortho.wait()
    up[...] = (math.sqrt(M * N / R) * dot3(nb[...], ortho[...], ((1,), (1,)))).astype(BF16)
    out.append(copy(6, up, up_out))
    for c in out:
        c.wait()


def shards(momentum, gradient, basis):
    hbm = pl.BlockSpec(memory_space=pltpu.HBM)
    v = lambda *s: pltpu.VMEM(s, F32)
    d = pltpu.SemaphoreType.DMA
    sems = []
    for n in (0, 7, 7, 8, 3, 7, 7, 8, 3, 7, 7, 3, 3, 7, 3, 3, 7, 15):
        sems += [d(()) if n == 0 else d((n,))] * 2
    out = jax.ShapeDtypeStruct
    nm, right, ortho, norms = pl.pallas_call(
        kernel,
        out_shape=(out((COLS, ROWS), F32), out((COLS, R), F32), out((ROWS, R), F32), out((8, R), F32)),
        in_specs=[hbm] * 3,
        out_specs=(hbm,) * 4,
        scratch_shapes=[
            v(COLS, ROWS), v(COLS, R), v(ROWS, R), v(8, R),
            v(COLS, ROWS), pltpu.VMEM((COLS, ROWS), BF16), v(COLS, R),
            v(COLS, ROWS), v(ROWS, R), v(128, R), v(128, R), v(7, 16, R), v(ROWS, R),
            v(R, R), v(NX, 16, R), v(NY, 16, R), v(R, R),
            v(COLS, R), v(3, FIRST, R), v(FIRST, R), v(7, SMALL, R), v(7, SECOND, R), v(SECOND, R),
            v(3, 8, R), v(NX, 8, R), v(COLS, R),
            v(R, 2 * R), v(2 * NZ, 1, R),
            *sems, d((3,)), d((4,)),
        ],
        compiler_params=pltpu.CompilerParams(
            collective_id=0, has_side_effects=True, vmem_limit_bytes=58 << 20
        ),
    )(momentum.T, gradient.T, basis)
    nm, nb, up = pl.pallas_call(
        finish,
        out_shape=(out((COLS, ROWS), F32), out((COLS, R), F32), out((COLS, ROWS), BF16)),
        in_specs=[hbm] * 4,
        out_specs=(hbm,) * 3,
        scratch_shapes=[v(COLS, ROWS), v(COLS, R), v(ROWS, R), v(8, R), v(COLS, R), pltpu.VMEM((COLS, ROWS), BF16), d((7,))],
        compiler_params=pltpu.CompilerParams(vmem_limit_bytes=58 << 20),
    )(nm, right, ortho, norms)
    return nm.T, nb, up.T


def solution(mesh):
    return jax.shard_map(
        shards,
        mesh=mesh,
        in_specs=(P("row", "col"), P("row", "col"), P("col", None)),
        out_specs=(P("row", "col"), P("col", None), P("row", "col")),
        check_vma=False,
    )
```

```python
import functools
import math

import jax
import jax.numpy as jnp
from jax import lax
from jax.experimental import pallas as pl
from jax.experimental.pallas import tpu as pltpu
from jax.sharding import PartitionSpec as P

M = 8192
N = 13312
R = 256
KEEP_RATE = 0.95
NORM_EPS = 1e-06

NX, NY, NZ = 4, 8, 8
ROWS = M // (NX * NY)
COLS = N // (2 * NZ)
CUT = 512
FIRST = CUT // NX
SMALL = FIRST // NY
SECOND = (COLS - CUT) // NY
PANEL = 32
KEPT = ((0, COLS), (COLS, COLS), (2 * COLS, ROWS), (2 * COLS + ROWS, 8))
FAR = (4, 3, 5, 2, 6, 1, 7)
NEAR = (1, 7, 2, 6, 3, 5, 4)
FAR_X = (2, 1, 3)
F32 = jnp.float32
BF16 = jnp.bfloat16
MESH = pl.DeviceIdType.MESH


def dot(a, b, dims):
    return lax.dot_general(
        a, b, (dims, ((), ())), precision=lax.Precision.HIGHEST, preferred_element_type=F32
    )


def dot3(a, b, dims):
    ah = a.astype(BF16)
    bh = b.astype(BF16)
    al = (a - ah.astype(F32)).astype(BF16)
    bl = (b - bh.astype(F32)).astype(BF16)
    one = lambda p, q: lax.dot_general(p, q, (dims, ((), ())), preferred_element_type=F32)
    return one(ah, bh) + (one(ah, bl) + one(al, bh))


def factor_panel(k, a):
    off = pl.multiple_of(k * PANEL, PANEL)
    base = pl.multiple_of(off // 128 * 128, 128)
    tiles = PANEL // 8
    sub = lax.broadcasted_iota(jnp.int32, (8, 128), 0)
    t = []
    for i in range(tiles):
        r = pl.ds(pl.multiple_of(off + 8 * i, 8), 8)
        row = a[r, :]
        own = pltpu.roll(a[r, pl.ds(base, 128)], lax.rem(128 - (off - base), 128), 1)
        t.append([own] + [row[:, 128 * q : 128 * q + 128] for q in range(4)])
    for b in range(tiles):
        cols = {}
        for i in range(b, tiles):
            for j in range(8):
                cols[i, j] = jnp.broadcast_to(t[i][0][:, 8 * b + j : 8 * b + j + 1], (8, 128))
        s = {}
        for j in range(8):
            for i in range(j, 8):
                s[i, j] = jnp.broadcast_to(cols[b, j][i : i + 1, :], (8, 128))
        scale = None
        for j in range(8):
            d = lax.rsqrt(s[j, j])
            l = {i: s[i, j] * d for i in range(j + 1, 8)}
            for m in range(j + 1, 8):
                for i in range(m, 8):
                    s[i, m] = s[i, m] - l[i] * l[m]
            pivot = [jnp.broadcast_to(t[b][q][j : j + 1, :], (8, 128)) * d for q in range(5)]
            for i in range(b, tiles):
                cols[i, j] = cols[i, j] * d
                for m in range(j + 1, 8):
                    cols[i, m] = cols[i, m] - cols[i, j] * l[m]
                times = cols[i, j] if i > b else jnp.where(sub > j, cols[i, j], 0.0)
                for q in range(5):
                    t[i][q] = t[i][q] - times * pivot[q]
            scale = d if j == 0 else jnp.where(sub == j, d, scale)
        for q in range(1, 5):
            t[b][q] = t[b][q] * scale
    r = jnp.concatenate([jnp.concatenate(t[i][1:], axis=1) for i in range(tiles)], axis=0)
    a[pl.ds(off, PANEL), R:] = r[:, R:]
    hi = r.astype(BF16).astype(F32)
    mi = (r - hi).astype(BF16).astype(F32)
    lo = r - hi - mi
    below = lax.broadcasted_iota(jnp.int32, (PANEL, R), 1) >= off + PANEL
    hl, ml, ll = (jnp.where(below, v[:, :R], 0.0).astype(BF16) for v in (hi, mi, lo))
    hr, mr, lr = hi.astype(BF16), mi.astype(BF16), lo.astype(BF16)
    lhs = jnp.concatenate([hl, hl, ml, ml, hl, ll], axis=0)
    rhs = jnp.concatenate([hr, mr, hr, mr, lr, hr], axis=0)
    a[...] = a[...] - lax.dot_general(
        lhs, rhs, (((0,), (0,)), ((), ())), preferred_element_type=F32
    )


def kernel(
    mom_hbm, grad_hbm, basis_hbm,
    out_ref,
    mom_ref, grad_ref, basis_ref, buf, part, core_in, half, z_in, power,
    gram, gx, gy, gram_all,
    wt, wx1_in, sx1, wy1_in, wy2_in, sy2, wx2_in, wx3_in, wf,
    a, sq,
    s_core, r_core, s_zr, r_zr, s_zg, r_zg, s_cg, r_cg,
    s_gx, r_gx, s_gy, r_gy, s_gz, r_gz, s_gc, r_gc,
    s_x1, r_x1, s_y1, r_y1, s_y2, r_y2, s_x2, r_x2, s_x3, r_x3,
    s_y1g, r_y1g, s_x1g, r_x1g, s_x2g, r_x2g, s_y2g, r_y2g,
    s_sq, r_sq, s_in,
):
    nm_ref, right_ref, ortho_ref, norms_ref = (out_ref.at[pl.ds(at, n), :] for at, n in KEPT)
    loads = [
        pltpu.make_async_copy(src, dst, s_in.at[i])
        for i, (src, dst) in enumerate(((mom_hbm, mom_ref), (grad_hbm, grad_ref), (basis_hbm, basis_ref)))
    ]
    for load in loads:
        load.start()
    row = lax.axis_index("row")
    col = lax.axis_index("col")
    x, y = row // NY, lax.rem(row, NY)
    z, core = col // 2, lax.rem(col, 2)

    def x_peer(k):
        xt = lax.rem(x + k, NX)
        return xt, (xt * NY + y, col)

    def y_peer(k):
        yt = lax.rem(y + k, NY)
        return yt, (x * NY + yt, col)

    def z_peer(k):
        zt = lax.rem(z + k, NZ)
        return zt, (row, zt * 2 + core)

    sibling = (row, z * 2 + 1 - core)

    def col_peer(k):
        return (row, lax.rem(col + k, 2 * NZ))

    sent = []

    def send(src, dst, ssem, rsem, dev):
        copy = pltpu.make_async_remote_copy(
            src_ref=src, dst_ref=dst, send_sem=ssem, recv_sem=rsem,
            device_id=dev, device_id_type=MESH,
        )
        copy.start()
        sent.append(copy)
        return copy

    def rows8(start, n):
        return pl.ds(pl.multiple_of(start, 8), n)

    barrier = pltpu.get_barrier_semaphore()
    peers = [x_peer(k)[1] for k in range(1, NX)]
    peers += [y_peer(k)[1] for k in range(1, NY)]
    peers += [col_peer(k) for k in range(1, 2 * NZ)]
    for dev in peers:
        pl.semaphore_signal(barrier, inc=1, device_id=dev, device_id_type=MESH)

    ii = lax.broadcasted_iota(jnp.int32, (R, R), 0)
    jj = lax.broadcasted_iota(jnp.int32, (R, R), 1)
    a[:, R:] = jnp.where(ii == jj, 1.0, 0.0).astype(F32)

    mine128 = rows8(core * 128, 128)
    theirs128 = rows8((1 - core) * 128, 128)
    mine16 = rows8(core * 128 + z * 16, 16)

    def part_power(half_core):
        lanes = pl.ds(pl.multiple_of(half_core * 128, 128), 128)
        return dot(buf[:, lanes], basis_ref[...], ((0,), (0,)))

    def send_all(order, peer, src, dst, ss, rr):
        out = {}
        for k in order:
            at, dev = peer(k)
            out[k] = send(src(at), dst(k), ss.at[k - 1], rr.at[k - 1], dev)
        return out

    with jax.named_scope("partial_power"):
        for load in loads:
            load.wait()
        buf[...] = mom_ref[...] + grad_ref[...].astype(F32)
        part[theirs128, :] = part_power(1 - core)
        pl.semaphore_wait(barrier, len(peers))
        c = send(part.at[theirs128, :], core_in, s_core, r_core, sibling)
        part[mine128, :] = part_power(core)

    with jax.named_scope("power_sum"):
        c.wait_recv()
        half[...] = part[mine128, :] + core_in[...]
        cs = send_all(FAR, z_peer, lambda zt: half.at[rows8(zt * 16, 16), :], lambda k: z_in.at[k - 1], s_zr, r_zr)
        total = half[rows8(z * 16, 16), :]
        for k in NEAR:
            cs[k].wait_recv()
            total = total + z_in[k - 1]

    def gather_z(ref, ss, rr, sc, rc):
        mine = ref.at[mine16, :]
        cs = send_all(FAR, z_peer, lambda zt: mine, lambda k: mine, ss, rr)
        return cs, [send(mine, mine, sc.at[0], rc.at[0], sibling)]

    def gather_core(ref, cs, fs, sc, rc):
        for k in NEAR:
            cs[k].wait_recv()
            zs = lax.rem(z + NZ - k, NZ)
            theirs = ref.at[rows8(core * 128 + zs * 16, 16), :]
            fs.append(send(theirs, theirs, sc.at[k], rc.at[k], sibling))

    with jax.named_scope("power_gather"):
        power[mine16, :] = total
        cs, fs = gather_z(power, s_zg, r_zg, s_cg, r_cg)
        gather_core(power, cs, fs, s_cg, r_cg)
        for c in fs:
            c.wait_recv()

    with jax.named_scope("w_dot"):
        wt[:CUT] = dot(buf[:CUT], power[...], ((1,), (0,)))
        c_x1 = send_all(FAR_X, x_peer, lambda xt: wt.at[rows8(xt * FIRST, FIRST), :], lambda k: wx1_in.at[k - 1], s_x1, r_x1)
        wt[CUT:] = dot(buf[CUT:], power[...], ((1,), (0,)))
        c_y2 = send_all(
            FAR, y_peer, lambda yt: wt.at[rows8(CUT + yt * SECOND, SECOND), :], lambda k: wy2_in.at[k - 1], s_y2, r_y2
        )

    with jax.named_scope("gram_dot"):
        gram[...] = dot(power[...], power[...], ((0,), (0,)))
        gx[x] = gram[mine16, :]
        c_gx = send_all(FAR_X, x_peer, lambda xt: gx.at[x], lambda k: gx.at[x], s_gx, r_gx)

    with jax.named_scope("gram_x"):
        for c in c_gx.values():
            c.wait_recv()
        gy[y] = (gx[0] + gx[1]) + (gx[2] + gx[3])
        c_gy = send_all(FAR, y_peer, lambda yt: gy.at[y], lambda k: gy.at[y], s_gy, r_gy)

    with jax.named_scope("w1_x"):
        for c in c_x1.values():
            c.wait_recv()
        sx1[...] = (wt[rows8(x * FIRST, FIRST), :] + wx1_in[0]) + (wx1_in[1] + wx1_in[2])
        c_y1 = send_all(FAR, y_peer, lambda yt: sx1.at[rows8(yt * SMALL, SMALL), :], lambda k: wy1_in.at[k - 1], s_y1, r_y1)

    with jax.named_scope("w2_y"):
        for c in c_y2.values():
            c.wait_recv()
        acc = wt[rows8(CUT + y * SECOND, SECOND), :]
        for k in range(NY - 1):
            acc = acc + wy2_in[k]
        sy2[...] = acc
        wx3_in[x] = acc[32:]
        c_x2 = send_all(FAR_X, x_peer, lambda xt: sy2.at[rows8(xt * 8, 8), :], lambda k: wx2_in.at[k - 1], s_x2, r_x2)
        c_x3 = send_all(FAR_X, x_peer, lambda xt: sy2.at[pl.ds(32, 8), :], lambda k: wx3_in.at[x], s_x3, r_x3)

    with jax.named_scope("gram_y"):
        for c in c_gy.values():
            c.wait_recv()
        gram_all[mine16, :] = ((gy[0] + gy[1]) + (gy[2] + gy[3])) + ((gy[4] + gy[5]) + (gy[6] + gy[7]))
        c_gz, fs = gather_z(gram_all, s_gz, r_gz, s_gc, r_gc)

    with jax.named_scope("w2_x"):
        for c in (*c_x2.values(), *c_x3.values()):
            c.wait_recv()
        w2 = wf.at[rows8(CUT + y * SECOND + x * 8, 8), :]
        w2[...] = (sy2[rows8(x * 8, 8), :] + wx2_in[0]) + (wx2_in[1] + wx2_in[2])
        c_x2g = send_all(FAR_X, x_peer, lambda xt: w2, lambda k: w2, s_x2g, r_x2g)
        wf[rows8(CUT + y * SECOND + 32, 8), :] = (wx3_in[0] + wx3_in[1]) + (wx3_in[2] + wx3_in[3])
    with jax.named_scope("w1_y"):
        for c in c_y1.values():
            c.wait_recv()
        acc = sx1[rows8(y * SMALL, SMALL), :]
        for k in range(NY - 1):
            acc = acc + wy1_in[k]
        w1 = wf.at[rows8(x * FIRST + y * SMALL, SMALL), :]
        w1[...] = acc
        c_y1g = send_all(FAR, y_peer, lambda yt: w1, lambda k: w1, s_y1g, r_y1g)

    with jax.named_scope("gram_z"):
        gather_core(gram_all, c_gz, fs, s_gc, r_gc)

    def factor(lo, hi):
        def body(k, carry):
            factor_panel(k, a)
            return carry
        lax.fori_loop(lo, hi, body, 0)

    with jax.named_scope("w2_x_gather"):
        for c in c_x2g.values():
            c.wait_recv()
        w2y = wf.at[rows8(CUT + y * SECOND, SECOND), :]
        c_y2g = send_all(FAR, y_peer, lambda yt: w2y, lambda k: w2y, s_y2g, r_y2g)

    with jax.named_scope("factor_first"):
        for c in fs:
            c.wait_recv()
        a[:, :R] = gram_all[...]
        factor(0, 2)

    with jax.named_scope("w1_y_gather"):
        for c in c_y1g.values():
            c.wait_recv()
        w1x = wf.at[rows8(x * FIRST, FIRST), :]
        c_x1g = send_all(FAR_X, x_peer, lambda xt: w1x, lambda k: w1x, s_x1g, r_x1g)

    with jax.named_scope("factor_rest"):
        factor(2, R // PANEL)

    with jax.named_scope("ortho"):
        ortho_ref[...] = dot3(power[...], a[:, R:], ((1,), (1,)))
    with jax.named_scope("right"):
        for c in c_x1g.values():
            c.wait_recv()
        right_ref[:CUT] = dot3(wf[:CUT], a[:, R:], ((1,), (1,)))
        for c in c_y2g.values():
            c.wait_recv()
        right_ref[CUT:] = dot3(wf[CUT:], a[:, R:], ((1,), (1,)))
    with jax.named_scope("squares"):
        rt = right_ref[...]
        sums = jnp.sum((rt * rt).reshape(COLS // 8, 8, R), axis=0)
        sq[col] = jnp.sum(sums, axis=0, keepdims=True)
        cs = [
            send(sq.at[col], sq.at[col], s_sq.at[k - 1], r_sq.at[k - 1], col_peer(k))
            for k in (8, 7, 9, 6, 10, 5, 11, 4, 12, 3, 13, 2, 14, 1, 15)
        ]

    with jax.named_scope("momentum"):
        nm_ref[...] = buf[...] - (1.0 - KEEP_RATE) * dot3(right_ref[...], ortho_ref[...], ((1,), (1,)))

    with jax.named_scope("norms"):
        for c in cs:
            c.wait_recv()
        squares = sq[0]
        for k in range(1, 2 * NZ):
            squares = squares + sq[k]
        norms_ref[...] = jnp.broadcast_to(jnp.sqrt(squares) + NORM_EPS, (8, R))

    with jax.named_scope("wait_sent"):
        for c in sent:
            c.wait_send()


def finish(kept, nm_out, nb_out, up_out, nb, up, sems):
    nm, right, ortho, norms = (kept.at[pl.ds(at, n), :] for at, n in KEPT)

    def copy(i, src, dst):
        c = pltpu.make_async_copy(src, dst, sems.at[i])
        c.start()
        return c

    out = [copy(0, nm, nm_out)]
    nb[...] = right[...] / norms[:1]
    out.append(copy(1, nb, nb_out))
    up[...] = (math.sqrt(M * N / R) * dot3(nb[...], ortho[...], ((1,), (1,)))).astype(BF16)
    out.append(copy(2, up, up_out))
    for c in out:
        c.wait()


def shards(momentum, gradient, basis):
    hbm = pl.BlockSpec(memory_space=pltpu.HBM)
    v = lambda *s: pltpu.VMEM(s, F32)
    d = pltpu.SemaphoreType.DMA
    sems = []
    for n in (0, 7, 7, 8, 3, 7, 7, 8, 3, 7, 7, 3, 3, 7, 3, 3, 7, 15):
        sems += [d(()) if n == 0 else d((n,))] * 2
    out = jax.ShapeDtypeStruct
    vmem = pl.BlockSpec(memory_space=pltpu.VMEM)
    kept = pl.pallas_call(
        kernel,
        out_shape=out((2 * COLS + ROWS + 8, R), F32),
        in_specs=[hbm] * 3,
        out_specs=vmem,
        scratch_shapes=[
            v(COLS, ROWS), pltpu.VMEM((COLS, ROWS), BF16), v(COLS, R),
            v(COLS, ROWS), v(ROWS, R), v(128, R), v(128, R), v(7, 16, R), v(ROWS, R),
            v(R, R), v(NX, 16, R), v(NY, 16, R), v(R, R),
            v(COLS, R), v(3, FIRST, R), v(FIRST, R), v(7, SMALL, R), v(7, SECOND, R), v(SECOND, R),
            v(3, 8, R), v(NX, 8, R), v(COLS, R),
            v(R, 2 * R), v(2 * NZ, 1, R),
            *sems, d((3,)),
        ],
        compiler_params=pltpu.CompilerParams(
            collective_id=0, has_side_effects=True, vmem_limit_bytes=40 << 20
        ),
    )(*(pltpu.with_memory_space_constraint(v, pltpu.HBM) for v in (momentum.T, gradient.T, basis)))
    nm, nb, up = pl.pallas_call(
        finish,
        out_shape=(out((COLS, ROWS), F32), out((COLS, R), F32), out((COLS, ROWS), BF16)),
        in_specs=[vmem],
        out_specs=(hbm,) * 3,
        scratch_shapes=[v(COLS, R), pltpu.VMEM((COLS, ROWS), BF16), d((3,))],
        compiler_params=pltpu.CompilerParams(vmem_limit_bytes=40 << 20),
    )(kept)
    return nm.T, nb, up.T


def solution(mesh):
    return jax.shard_map(
        shards,
        mesh=mesh,
        in_specs=(P("row", "col"), P("row", "col"), P("col", None)),
        out_specs=(P("row", "col"), P("col", None), P("row", "col")),
        check_vma=False,
    )
```

```python
import functools
import math

import jax
import jax.numpy as jnp
from jax import lax
from jax.experimental import pallas as pl
from jax.experimental.pallas import tpu as pltpu
from jax.sharding import PartitionSpec as P

M = 8192
N = 13312
R = 256
KEEP_RATE = 0.95
NORM_EPS = 1e-06

NX, NY, NZ = 4, 8, 8
ROWS = M // (NX * NY)
COLS = N // (2 * NZ)
CUT = (512, 768)
FIRST = tuple(n // NX for n in CUT)
SMALL = tuple(n // NY for n in FIRST)
SECOND = tuple((COLS - n) // NY for n in CUT)
PANEL = 32
KEPT = ((0, COLS), (COLS, COLS), (2 * COLS, ROWS), (2 * COLS + ROWS, 8))
FAR = (4, 3, 5, 2, 6, 1, 7)
NEAR = (1, 7, 2, 6, 3, 5, 4)
FAR_X = (2, 1, 3)
HALVES = (0, 1)
F32 = jnp.float32
BF16 = jnp.bfloat16
MESH = pl.DeviceIdType.MESH


def dot(a, b, dims):
    return lax.dot_general(
        a, b, (dims, ((), ())), precision=lax.Precision.HIGHEST, preferred_element_type=F32
    )


def dot3(a, b, dims):
    ah = a.astype(BF16)
    bh = b.astype(BF16)
    al = (a - ah.astype(F32)).astype(BF16)
    bl = (b - bh.astype(F32)).astype(BF16)
    one = lambda p, q: lax.dot_general(p, q, (dims, ((), ())), preferred_element_type=F32)
    return one(ah, bh) + (one(ah, bl) + one(al, bh))


def factor_panel(k, a):
    off = pl.multiple_of(k * PANEL, PANEL)
    base = pl.multiple_of(off // 128 * 128, 128)
    tiles = PANEL // 8
    sub = lax.broadcasted_iota(jnp.int32, (8, 128), 0)
    t = []
    for i in range(tiles):
        r = pl.ds(pl.multiple_of(off + 8 * i, 8), 8)
        row = a[r, :]
        own = pltpu.roll(a[r, pl.ds(base, 128)], lax.rem(128 - (off - base), 128), 1)
        t.append([own] + [row[:, 128 * q : 128 * q + 128] for q in range(4)])
    for b in range(tiles):
        cols = {}
        for i in range(b, tiles):
            for j in range(8):
                cols[i, j] = jnp.broadcast_to(t[i][0][:, 8 * b + j : 8 * b + j + 1], (8, 128))
        s = {}
        for j in range(8):
            for i in range(j, 8):
                s[i, j] = jnp.broadcast_to(cols[b, j][i : i + 1, :], (8, 128))
        scale = None
        for j in range(8):
            d = lax.rsqrt(s[j, j])
            l = {i: s[i, j] * d for i in range(j + 1, 8)}
            for m in range(j + 1, 8):
                for i in range(m, 8):
                    s[i, m] = s[i, m] - l[i] * l[m]
            pivot = [jnp.broadcast_to(t[b][q][j : j + 1, :], (8, 128)) * d for q in range(5)]
            for i in range(b, tiles):
                cols[i, j] = cols[i, j] * d
                for m in range(j + 1, 8):
                    cols[i, m] = cols[i, m] - cols[i, j] * l[m]
                times = cols[i, j] if i > b else jnp.where(sub > j, cols[i, j], 0.0)
                for q in range(5):
                    t[i][q] = t[i][q] - times * pivot[q]
            scale = d if j == 0 else jnp.where(sub == j, d, scale)
        for q in range(1, 5):
            t[b][q] = t[b][q] * scale
    r = jnp.concatenate([jnp.concatenate(t[i][1:], axis=1) for i in range(tiles)], axis=0)
    a[pl.ds(off, PANEL), R:] = r[:, R:]
    hi = r.astype(BF16).astype(F32)
    mi = (r - hi).astype(BF16).astype(F32)
    lo = r - hi - mi
    below = lax.broadcasted_iota(jnp.int32, (PANEL, R), 1) >= off + PANEL
    hl, ml, ll = (jnp.where(below, v[:, :R], 0.0).astype(BF16) for v in (hi, mi, lo))
    hr, mr, lr = hi.astype(BF16), mi.astype(BF16), lo.astype(BF16)
    lhs = jnp.concatenate([hl, hl, ml, ml, hl, ll], axis=0)
    rhs = jnp.concatenate([hr, mr, hr, mr, lr, hr], axis=0)
    a[...] = a[...] - lax.dot_general(
        lhs, rhs, (((0,), (0,)), ((), ())), preferred_element_type=F32
    )


def kernel(
    mom_hbm, grad_hbm, basis_hbm,
    out_ref,
    mom_ref, grad_ref, basis_ref, buf, part, core_in, half, z_in, power,
    gram, gx, gy, gram_all,
    wt, wx1_in, sx1, wy1_in, wy2_in, sy2, wx2_in, wx3_in, wf,
    a, sq,
    s_core, r_core, s_zr, r_zr, s_zg, r_zg, s_cg, r_cg,
    s_gx, r_gx, s_gy, r_gy, s_gz, r_gz, s_gc, r_gc,
    s_x1, r_x1, s_y1, r_y1, s_y2, r_y2, s_x2, r_x2, s_x3, r_x3,
    s_y1g, r_y1g, s_x1g, r_x1g, s_x2g, r_x2g, s_y2g, r_y2g,
    s_sq, r_sq, s_in,
):
    nm_ref, right_ref, ortho_ref, norms_ref = (out_ref.at[pl.ds(at, n), :] for at, n in KEPT)
    loads = [
        pltpu.make_async_copy(src, dst, s_in.at[i])
        for i, (src, dst) in enumerate(((mom_hbm, mom_ref), (grad_hbm, grad_ref), (basis_hbm, basis_ref)))
    ]
    for load in loads:
        load.start()
    row = lax.axis_index("row")
    col = lax.axis_index("col")
    x, y = row // NY, lax.rem(row, NY)
    z, core = col // 2, lax.rem(col, 2)

    def x_peer(k):
        xt = lax.rem(x + k, NX)
        return xt, (xt * NY + y, col)

    def y_peer(k):
        yt = lax.rem(y + k, NY)
        return yt, (x * NY + yt, col)

    def z_peer(k):
        zt = lax.rem(z + k, NZ)
        return zt, (row, zt * 2 + core)

    sibling = (row, z * 2 + 1 - core)

    def col_peer(k):
        return (row, lax.rem(col + k, 2 * NZ))

    sent = []

    def send(src, dst, ssem, rsem, dev):
        copy = pltpu.make_async_remote_copy(
            src_ref=src, dst_ref=dst, send_sem=ssem, recv_sem=rsem,
            device_id=dev, device_id_type=MESH,
        )
        copy.start()
        sent.append(copy)
        return copy

    def rows8(start, n):
        return pl.ds(pl.multiple_of(start, 8), n)

    barrier = pltpu.get_barrier_semaphore()
    peers = [x_peer(k)[1] for k in range(1, NX)]
    peers += [y_peer(k)[1] for k in range(1, NY)]
    peers += [col_peer(k) for k in range(1, 2 * NZ)]
    for dev in peers:
        pl.semaphore_signal(barrier, inc=1, device_id=dev, device_id_type=MESH)

    ii = lax.broadcasted_iota(jnp.int32, (R, R), 0)
    jj = lax.broadcasted_iota(jnp.int32, (R, R), 1)
    a[:, R:] = jnp.where(ii == jj, 1.0, 0.0).astype(F32)

    mine128 = rows8(core * 128, 128)
    theirs128 = rows8((1 - core) * 128, 128)
    mine16 = rows8(core * 128 + z * 16, 16)

    def part_power(half_core):
        lanes = pl.ds(pl.multiple_of(half_core * 128, 128), 128)
        return dot(buf[:, lanes], basis_ref[...], ((0,), (0,)))

    def send_all(order, peer, src, dst, ss, rr):
        out = {}
        for k in order:
            at, dev = peer(k)
            out[k] = send(src(at), dst(k), ss.at[k - 1], rr.at[k - 1], dev)
        return out

    def arrive(copies):
        for c in copies.values():
            c.wait_recv()

    with jax.named_scope("partial_power"):
        for load in loads:
            load.wait()
        buf[...] = mom_ref[...] + grad_ref[...].astype(F32)
        theirs = part_power(1 - core)
        for h in HALVES:
            part[h, theirs128, :] = theirs[:, 128 * h : 128 * h + 128]
        pl.semaphore_wait(barrier, len(peers))
        c_core = [send(part.at[h, theirs128, :], core_in.at[h], s_core.at[h], r_core.at[h], sibling) for h in HALVES]
        mine = part_power(core)

    c_z = [None, None]
    with jax.named_scope("power_core"):
        for h in HALVES:
            c_core[h].wait_recv()
            half[h] = mine[:, 128 * h : 128 * h + 128] + core_in[h]
            c_z[h] = send_all(
                FAR, z_peer, lambda zt: half.at[h, rows8(zt * 16, 16), :], lambda k: z_in.at[h, k - 1], s_zr.at[h], r_zr.at[h]
            )

    def gather_z(ref, ss, rr, sc, rc):
        own = ref.at[mine16, :]
        cs = send_all(FAR, z_peer, lambda zt: own, lambda k: own, ss, rr)
        return cs, [send(own, own, sc.at[0], rc.at[0], sibling)]

    def gather_core(ref, cs, fs, sc, rc):
        for k in NEAR:
            cs[k].wait_recv()
            zs = lax.rem(z + NZ - k, NZ)
            other = ref.at[rows8(core * 128 + zs * 16, 16), :]
            fs.append(send(other, other, sc.at[k], rc.at[k], sibling))

    c_zg, f_zg = [None, None], [None, None]
    with jax.named_scope("power_z"):
        for h in HALVES:
            total = half[h, rows8(z * 16, 16), :]
            for k in NEAR:
                c_z[h][k].wait_recv()
                total = total + z_in[h, k - 1]
            power[h, mine16, :] = total
            c_zg[h], f_zg[h] = gather_z(power.at[h], s_zg.at[h], r_zg.at[h], s_cg.at[h], r_cg.at[h])

    def w_first(h):
        wt[h, : CUT[h]] = dot(buf[: CUT[h]], power[h], ((1,), (0,)))
        n = FIRST[h]
        return send_all(
            FAR_X, x_peer, lambda xt: wt.at[h, rows8(xt * n, n), :], lambda k: wx1_in.at[h, k - 1, pl.ds(0, n), :],
            s_x1.at[h], r_x1.at[h],
        )

    def w_second_dot(h):
        wt[h, CUT[h] :] = dot(buf[CUT[h] :], power[h], ((1,), (0,)))

    def w_second(h):
        n = SECOND[h]
        return send_all(
            FAR, y_peer, lambda yt: wt.at[h, rows8(CUT[h] + yt * n, n), :], lambda k: wy2_in.at[h, k - 1, pl.ds(0, n), :],
            s_y2.at[h], r_y2.at[h],
        )

    def w1_x(h, got):
        arrive(got)
        n, m = FIRST[h], SMALL[h]
        sx1[h, :n] = (wt[h, rows8(x * n, n), :] + wx1_in[h, 0, :n]) + (wx1_in[h, 1, :n] + wx1_in[h, 2, :n])
        return send_all(
            FAR, y_peer, lambda yt: sx1.at[h, rows8(yt * m, m), :], lambda k: wy1_in.at[h, k - 1, pl.ds(0, m), :],
            s_y1.at[h], r_y1.at[h],
        )

    def w2_y(h, got):
        arrive(got)
        n = SECOND[h]
        acc = wt[h, rows8(CUT[h] + y * n, n), :]
        for k in range(NY - 1):
            acc = acc + wy2_in[h, k, :n]
        sy2[h, :n] = acc
        wx3_in[h, x] = acc[n - 8 :]
        one = {}
        if n > 8:
            one = send_all(
                FAR_X, x_peer, lambda xt: sy2.at[h, rows8(xt * 8, 8), :], lambda k: wx2_in.at[h, k - 1], s_x2.at[h], r_x2.at[h]
            )
        two = send_all(
            FAR_X, x_peer, lambda xt: sy2.at[h, pl.ds(n - 8, 8), :], lambda k: wx3_in.at[h, x], s_x3.at[h], r_x3.at[h]
        )
        return one, two

    def w1_y(h, got):
        arrive(got)
        n, m = FIRST[h], SMALL[h]
        acc = sx1[h, rows8(y * m, m), :]
        for k in range(NY - 1):
            acc = acc + wy1_in[h, k, :m]
        own = wf.at[h, rows8(x * n + y * m, m), :]
        own[...] = acc
        return send_all(FAR, y_peer, lambda yt: own, lambda k: own, s_y1g.at[h], r_y1g.at[h])

    def w2_x(h, got):
        arrive(got[0])
        arrive(got[1])
        n = SECOND[h]
        wf[h, rows8(CUT[h] + y * n + n - 8, 8), :] = (wx3_in[h, 0] + wx3_in[h, 1]) + (wx3_in[h, 2] + wx3_in[h, 3])
        if n == 8:
            return {}
        own = wf.at[h, rows8(CUT[h] + y * n + x * 8, 8), :]
        own[...] = (sy2[h, rows8(x * 8, 8), :] + wx2_in[h, 0]) + (wx2_in[h, 1] + wx2_in[h, 2])
        return send_all(FAR_X, x_peer, lambda xt: own, lambda k: own, s_x2g.at[h], r_x2g.at[h])

    def w2_x_gather(h, got):
        arrive(got)
        own = wf.at[h, rows8(CUT[h] + y * SECOND[h], SECOND[h]), :]
        return send_all(FAR, y_peer, lambda yt: own, lambda k: own, s_y2g.at[h], r_y2g.at[h])

    def w1_y_gather(h, got):
        arrive(got)
        own = wf.at[h, rows8(x * FIRST[h], FIRST[h]), :]
        return send_all(FAR_X, x_peer, lambda xt: own, lambda k: own, s_x1g.at[h], r_x1g.at[h])

    def factor(lo, hi):
        def body(k, carry):
            factor_panel(k, a)
            return carry
        lax.fori_loop(lo, hi, body, 0)

    with jax.named_scope("first_half"):
        gather_core(power.at[0], c_zg[0], f_zg[0], s_cg.at[0], r_cg.at[0])
        for c in f_zg[0]:
            c.wait_recv()
        x1_0 = w_first(0)
        w_second_dot(0)
        y2_0 = w_second(0)
        gather_core(power.at[1], c_zg[1], f_zg[1], s_cg.at[1], r_cg.at[1])
        for c in f_zg[1]:
            c.wait_recv()

    with jax.named_scope("gram_dot"):
        whole = jnp.concatenate([power[0], power[1]], axis=1)
        gram[...] = dot(whole, whole, ((0,), (0,)))
        gx[x] = gram[mine16, :]
        c_gx = send_all(FAR_X, x_peer, lambda xt: gx.at[x], lambda k: gx.at[x], s_gx, r_gx)

    with jax.named_scope("second_half"):
        x1_1 = w_first(1)
        w_second_dot(1)
        y1_0 = w1_x(0, x1_0)

    with jax.named_scope("gram_x"):
        arrive(c_gx)
        gy[y] = (gx[0] + gx[1]) + (gx[2] + gx[3])
        c_gy = send_all(FAR, y_peer, lambda yt: gy.at[y], lambda k: gy.at[y], s_gy, r_gy)

    with jax.named_scope("w_sums"):
        y2_1 = w_second(1)
        x2_0 = w2_y(0, y2_0)
        y1_1 = w1_x(1, x1_1)

    with jax.named_scope("gram_y"):
        arrive(c_gy)
        gram_all[mine16, :] = ((gy[0] + gy[1]) + (gy[2] + gy[3])) + ((gy[4] + gy[5]) + (gy[6] + gy[7]))
        c_gz, fs = gather_z(gram_all, s_gz, r_gz, s_gc, r_gc)

    with jax.named_scope("w_gathers"):
        y1g_0 = w1_y(0, y1_0)
        x2g_0 = w2_x(0, x2_0)
        x2_1 = w2_y(1, y2_1)
        y1g_1 = w1_y(1, y1_1)
        y2g_1 = w2_x_gather(1, w2_x(1, x2_1))

    with jax.named_scope("gram_z"):
        gather_core(gram_all, c_gz, fs, s_gc, r_gc)
        y2g_0 = w2_x_gather(0, x2g_0)
        for c in fs:
            c.wait_recv()
        a[:, :R] = gram_all[...]

    with jax.named_scope("factor_first"):
        x1g_0 = w1_y_gather(0, y1g_0)
        factor(0, 1)
    with jax.named_scope("w_last_gathers"):
        x1g_1 = w1_y_gather(1, y1g_1)
    with jax.named_scope("factor_rest"):
        factor(1, R // PANEL)

    with jax.named_scope("ortho"):
        ortho_ref[...] = dot3(jnp.concatenate([power[0], power[1]], axis=1), a[:, R:], ((1,), (1,)))
    with jax.named_scope("right"):
        arrive(x1g_0)
        arrive(x1g_1)
        right_ref[: CUT[0]] = dot3(jnp.concatenate([wf[0, : CUT[0]], wf[1, : CUT[0]]], axis=1), a[:, R:], ((1,), (1,)))
        arrive(y2g_0)
        arrive(y2g_1)
        right_ref[CUT[0] :] = dot3(jnp.concatenate([wf[0, CUT[0] :], wf[1, CUT[0] :]], axis=1), a[:, R:], ((1,), (1,)))
    with jax.named_scope("squares"):
        rt = right_ref[...]
        sums = jnp.sum((rt * rt).reshape(COLS // 8, 8, R), axis=0)
        sq[col] = jnp.sum(sums, axis=0, keepdims=True)
        cs = [
            send(sq.at[col], sq.at[col], s_sq.at[k - 1], r_sq.at[k - 1], col_peer(k))
            for k in (8, 7, 9, 6, 10, 5, 11, 4, 12, 3, 13, 2, 14, 1, 15)
        ]

    with jax.named_scope("momentum"):
        nm_ref[...] = buf[...] - (1.0 - KEEP_RATE) * dot3(right_ref[...], ortho_ref[...], ((1,), (1,)))

    with jax.named_scope("norms"):
        for c in cs:
            c.wait_recv()
        squares = sq[0]
        for k in range(1, 2 * NZ):
            squares = squares + sq[k]
        norms_ref[...] = jnp.broadcast_to(jnp.sqrt(squares) + NORM_EPS, (8, R))

    with jax.named_scope("wait_sent"):
        for c in sent:
            c.wait_send()


def finish(kept, nm_out, nb_out, up_out, nb, up, sems):
    nm, right, ortho, norms = (kept.at[pl.ds(at, n), :] for at, n in KEPT)

    def copy(i, src, dst):
        c = pltpu.make_async_copy(src, dst, sems.at[i])
        c.start()
        return c

    out = [copy(0, nm, nm_out)]
    nb[...] = right[...] / norms[:1]
    out.append(copy(1, nb, nb_out))
    up[...] = (math.sqrt(M * N / R) * dot3(nb[...], ortho[...], ((1,), (1,)))).astype(BF16)
    out.append(copy(2, up, up_out))
    for c in out:
        c.wait()


def shards(momentum, gradient, basis):
    hbm = pl.BlockSpec(memory_space=pltpu.HBM)
    v = lambda *s: pltpu.VMEM(s, F32)
    d = pltpu.SemaphoreType.DMA
    sems = []
    for n in (2, (2, 7), (2, 7), (2, 8), 3, 7, 7, 8, (2, 3), (2, 7), (2, 7), (2, 3), (2, 3), (2, 7), (2, 3), (2, 3), (2, 7), 15):
        sems += [d(n if isinstance(n, tuple) else (n,))] * 2
    out = jax.ShapeDtypeStruct
    vmem = pl.BlockSpec(memory_space=pltpu.VMEM)
    kept = pl.pallas_call(
        kernel,
        out_shape=out((2 * COLS + ROWS + 8, R), F32),
        in_specs=[hbm] * 3,
        out_specs=vmem,
        scratch_shapes=[
            v(COLS, ROWS), pltpu.VMEM((COLS, ROWS), BF16), v(COLS, R),
            v(COLS, ROWS), v(2, ROWS, 128), v(2, 128, 128), v(2, 128, 128), v(2, 7, 16, 128), v(2, ROWS, 128),
            v(R, R), v(NX, 16, R), v(NY, 16, R), v(R, R),
            v(2, COLS, 128), v(2, 3, FIRST[1], 128), v(2, FIRST[1], 128), v(2, 7, SMALL[1], 128),
            v(2, 7, SECOND[0], 128), v(2, SECOND[0], 128), v(2, 3, 8, 128), v(2, NX, 8, 128), v(2, COLS, 128),
            v(R, 2 * R), v(2 * NZ, 1, R),
            *sems, d((3,)),
        ],
        compiler_params=pltpu.CompilerParams(
            collective_id=0, has_side_effects=True, vmem_limit_bytes=40 << 20
        ),
    )(*(pltpu.with_memory_space_constraint(v, pltpu.HBM) for v in (momentum.T, gradient.T, basis)))
    nm, nb, up = pl.pallas_call(
        finish,
        out_shape=(out((COLS, ROWS), F32), out((COLS, R), F32), out((COLS, ROWS), BF16)),
        in_specs=[vmem],
        out_specs=(hbm,) * 3,
        scratch_shapes=[v(COLS, R), pltpu.VMEM((COLS, ROWS), BF16), d((3,))],
        compiler_params=pltpu.CompilerParams(vmem_limit_bytes=40 << 20),
    )(kept)
    return nm.T, nb, up.T


def solution(mesh):
    return jax.shard_map(
        shards,
        mesh=mesh,
        in_specs=(P("row", "col"), P("row", "col"), P("col", None)),
        out_specs=(P("row", "col"), P("col", None), P("row", "col")),
        check_vma=False,
    )
```

```python
import functools
import math

import jax
import jax.numpy as jnp
from jax import lax
from jax.experimental import pallas as pl
from jax.experimental.pallas import tpu as pltpu
from jax.sharding import PartitionSpec as P

M = 8192
N = 13312
R = 256
KEEP_RATE = 0.95
NORM_EPS = 1e-06

NX, NY, NZ = 4, 8, 8
ROWS = M // (NX * NY)
COLS = N // (2 * NZ)
CUT = (512, 768)
FIRST = tuple(n // NX for n in CUT)
SMALL = tuple(n // NY for n in FIRST)
SECOND = tuple((COLS - n) // NY for n in CUT)
PANEL = 32
KEPT = ((0, COLS), (COLS, COLS), (2 * COLS, ROWS), (2 * COLS + ROWS, 8))
FAR = (4, 3, 5, 2, 6, 1, 7)
NEAR = (1, 7, 2, 6, 3, 5, 4)
FAR_X = (2, 1, 3)
HALVES = (0, 1)
F32 = jnp.float32
BF16 = jnp.bfloat16
MESH = pl.DeviceIdType.MESH


def dot(a, b, dims):
    return lax.dot_general(
        a, b, (dims, ((), ())), precision=lax.Precision.HIGHEST, preferred_element_type=F32
    )


def dot3(a, b, dims):
    ah = a.astype(BF16)
    bh = b.astype(BF16)
    al = (a - ah.astype(F32)).astype(BF16)
    bl = (b - bh.astype(F32)).astype(BF16)
    one = lambda p, q: lax.dot_general(p, q, (dims, ((), ())), preferred_element_type=F32)
    return one(ah, bh) + (one(ah, bl) + one(al, bh))


def factor_panel(k, a, last=False):
    off = pl.multiple_of(k * PANEL, PANEL)
    base = pl.multiple_of(off // 128 * 128, 128)
    tiles = PANEL // 8
    sub = lax.broadcasted_iota(jnp.int32, (8, 128), 0)
    t = []
    for i in range(tiles):
        r = pl.ds(pl.multiple_of(off + 8 * i, 8), 8)
        row = a[r, :]
        own = pltpu.roll(a[r, pl.ds(base, 128)], lax.rem(128 - (off - base), 128), 1)
        t.append([own] + [row[:, 128 * q : 128 * q + 128] for q in range(4)])
    for b in range(tiles):
        cols = {}
        for i in range(b, tiles):
            for j in range(8):
                cols[i, j] = jnp.broadcast_to(t[i][0][:, 8 * b + j : 8 * b + j + 1], (8, 128))
        s = {}
        for j in range(8):
            for i in range(j, 8):
                s[i, j] = jnp.broadcast_to(cols[b, j][i : i + 1, :], (8, 128))
        scale = None
        for j in range(8):
            d = lax.rsqrt(s[j, j])
            l = {i: s[i, j] * d for i in range(j + 1, 8)}
            for m in range(j + 1, 8):
                for i in range(m, 8):
                    s[i, m] = s[i, m] - l[i] * l[m]
            pivot = [jnp.broadcast_to(t[b][q][j : j + 1, :], (8, 128)) * d for q in range(5)]
            for i in range(b, tiles):
                cols[i, j] = cols[i, j] * d
                for m in range(j + 1, 8):
                    cols[i, m] = cols[i, m] - cols[i, j] * l[m]
                times = cols[i, j] if i > b else jnp.where(sub > j, cols[i, j], 0.0)
                for q in range(5):
                    t[i][q] = t[i][q] - times * pivot[q]
            scale = d if j == 0 else jnp.where(sub == j, d, scale)
        for q in range(1, 5):
            t[b][q] = t[b][q] * scale
    r = jnp.concatenate([jnp.concatenate(t[i][1:], axis=1) for i in range(tiles)], axis=0)
    a[pl.ds(off, PANEL), R:] = r[:, R:]
    if last:
        return
    hi = r.astype(BF16).astype(F32)
    mi = (r - hi).astype(BF16).astype(F32)
    lo = r - hi - mi
    below = lax.broadcasted_iota(jnp.int32, (PANEL, R), 1) >= off + PANEL
    hl, ml, ll = (jnp.where(below, v[:, :R], 0.0).astype(BF16) for v in (hi, mi, lo))
    hr, mr, lr = hi.astype(BF16), mi.astype(BF16), lo.astype(BF16)
    lhs = jnp.concatenate([hl, hl, ml, ml, hl, ll], axis=0)
    rhs = jnp.concatenate([hr, mr, hr, mr, lr, hr], axis=0)
    a[...] = a[...] - lax.dot_general(
        lhs, rhs, (((0,), (0,)), ((), ())), preferred_element_type=F32
    )


def kernel(
    mom_hbm, grad_hbm, basis_hbm,
    out_ref,
    mom_ref, grad_ref, basis_ref, buf, part, core_in, half, z_in, power,
    gram, gx, gy, gram_all,
    wt, wx1_in, sx1, wy1_in, wy2_in, sy2, wx2_in, wx3_in, wf,
    a, sq,
    s_core, r_core, s_zr, r_zr, s_zg, r_zg, s_cg, r_cg,
    s_gx, r_gx, s_gy, r_gy, s_gz, r_gz, s_gc, r_gc,
    s_x1, r_x1, s_y1, r_y1, s_y2, r_y2, s_x2, r_x2, s_x3, r_x3,
    s_y1g, r_y1g, s_x1g, r_x1g, s_x2g, r_x2g, s_y2g, r_y2g,
    s_sq, r_sq, s_in,
):
    nm_ref, right_ref, ortho_ref, norms_ref = (out_ref.at[pl.ds(at, n), :] for at, n in KEPT)
    loads = [
        [
            pltpu.make_async_copy(src.at[pl.ds(at, COLS // 2), :], dst.at[pl.ds(at, COLS // 2), :], s_in.at[i, q])
            for i, (src, dst) in enumerate(((mom_hbm, mom_ref), (grad_hbm, grad_ref), (basis_hbm, basis_ref)))
        ]
        for q, at in enumerate((0, COLS // 2))
    ]
    for load in loads[0] + loads[1]:
        load.start()
    row = lax.axis_index("row")
    col = lax.axis_index("col")
    x, y = row // NY, lax.rem(row, NY)
    z, core = col // 2, lax.rem(col, 2)

    def x_peer(k):
        xt = lax.rem(x + k, NX)
        return xt, (xt * NY + y, col)

    def y_peer(k):
        yt = lax.rem(y + k, NY)
        return yt, (x * NY + yt, col)

    def z_peer(k):
        zt = lax.rem(z + k, NZ)
        return zt, (row, zt * 2 + core)

    sibling = (row, z * 2 + 1 - core)

    def col_peer(k):
        return (row, lax.rem(col + k, 2 * NZ))

    sent = []

    def send(src, dst, ssem, rsem, dev):
        copy = pltpu.make_async_remote_copy(
            src_ref=src, dst_ref=dst, send_sem=ssem, recv_sem=rsem,
            device_id=dev, device_id_type=MESH,
        )
        copy.start()
        sent.append(copy)
        return copy

    def rows8(start, n):
        return pl.ds(pl.multiple_of(start, 8), n)

    barrier = pltpu.get_barrier_semaphore()
    peers = [x_peer(k)[1] for k in range(1, NX)]
    peers += [y_peer(k)[1] for k in range(1, NY)]
    peers += [col_peer(k) for k in range(1, 2 * NZ)]
    for dev in peers:
        pl.semaphore_signal(barrier, inc=1, device_id=dev, device_id_type=MESH)

    ii = lax.broadcasted_iota(jnp.int32, (R, R), 0)
    jj = lax.broadcasted_iota(jnp.int32, (R, R), 1)
    a[:, R:] = jnp.where(ii == jj, 1.0, 0.0).astype(F32)

    mine128 = rows8(core * 128, 128)
    theirs128 = rows8((1 - core) * 128, 128)
    mine16 = rows8(core * 128 + z * 16, 16)

    def part_power(half_core, q):
        lanes = pl.ds(pl.multiple_of(half_core * 128, 128), 128)
        some = pl.ds(q * (COLS // 2), COLS // 2)
        return dot(buf[some, lanes], basis_ref[some, :], ((0,), (0,)))

    def send_all(order, peer, src, dst, ss, rr):
        out = {}
        for k in order:
            at, dev = peer(k)
            out[k] = send(src(at), dst(k), ss.at[k - 1], rr.at[k - 1], dev)
        return out

    def arrive(copies):
        for c in copies.values():
            c.wait_recv()

    with jax.named_scope("partial_power"):
        theirs, mine = [], []
        for q in range(2):
            for load in loads[q]:
                load.wait()
            some = pl.ds(q * (COLS // 2), COLS // 2)
            buf[some, :] = mom_ref[some, :] + grad_ref[some, :].astype(F32)
            theirs.append(part_power(1 - core, q))
            if q == 0:
                mine.append(part_power(core, q))
        theirs = theirs[0] + theirs[1]
        for h in HALVES:
            part[h, theirs128, :] = theirs[:, 128 * h : 128 * h + 128]
        pl.semaphore_wait(barrier, len(peers))
        c_core = [send(part.at[h, theirs128, :], core_in.at[h], s_core.at[h], r_core.at[h], sibling) for h in HALVES]
        mine = mine[0] + part_power(core, 1)

    c_z = [None, None]
    with jax.named_scope("power_core"):
        for h in HALVES:
            c_core[h].wait_recv()
            half[h] = mine[:, 128 * h : 128 * h + 128] + core_in[h]
            c_z[h] = send_all(
                FAR, z_peer, lambda zt: half.at[h, rows8(zt * 16, 16), :], lambda k: z_in.at[h, k - 1], s_zr.at[h], r_zr.at[h]
            )

    def gather_z(ref, ss, rr, sc, rc):
        own = ref.at[mine16, :]
        cs = send_all(FAR, z_peer, lambda zt: own, lambda k: own, ss, rr)
        return cs, [send(own, own, sc.at[0], rc.at[0], sibling)]

    def gather_core(ref, cs, fs, sc, rc):
        for k in NEAR:
            cs[k].wait_recv()
            zs = lax.rem(z + NZ - k, NZ)
            other = ref.at[rows8(core * 128 + zs * 16, 16), :]
            fs.append(send(other, other, sc.at[k], rc.at[k], sibling))

    c_zg, f_zg = [None, None], [None, None]
    with jax.named_scope("power_z"):
        for h in HALVES:
            total = half[h, rows8(z * 16, 16), :]
            for k in NEAR:
                c_z[h][k].wait_recv()
                total = total + z_in[h, k - 1]
            power[h, mine16, :] = total
            c_zg[h], f_zg[h] = gather_z(power.at[h], s_zg.at[h], r_zg.at[h], s_cg.at[h], r_cg.at[h])

    def w_first(h):
        wt[h, : CUT[h]] = dot(buf[: CUT[h]], power[h], ((1,), (0,)))
        n = FIRST[h]
        return send_all(
            FAR_X, x_peer, lambda xt: wt.at[h, rows8(xt * n, n), :], lambda k: wx1_in.at[h, k - 1, pl.ds(0, n), :],
            s_x1.at[h], r_x1.at[h],
        )

    def w_second_dot(h):
        wt[h, CUT[h] :] = dot(buf[CUT[h] :], power[h], ((1,), (0,)))

    def w_second(h):
        n = SECOND[h]
        return send_all(
            FAR, y_peer, lambda yt: wt.at[h, rows8(CUT[h] + yt * n, n), :], lambda k: wy2_in.at[h, k - 1, pl.ds(0, n), :],
            s_y2.at[h], r_y2.at[h],
        )

    def w1_x(h, got):
        arrive(got)
        n, m = FIRST[h], SMALL[h]
        sx1[h, :n] = (wt[h, rows8(x * n, n), :] + wx1_in[h, 0, :n]) + (wx1_in[h, 1, :n] + wx1_in[h, 2, :n])
        return send_all(
            FAR, y_peer, lambda yt: sx1.at[h, rows8(yt * m, m), :], lambda k: wy1_in.at[h, k - 1, pl.ds(0, m), :],
            s_y1.at[h], r_y1.at[h],
        )

    def w2_y(h, got):
        arrive(got)
        n = SECOND[h]
        acc = wt[h, rows8(CUT[h] + y * n, n), :]
        for k in range(NY - 1):
            acc = acc + wy2_in[h, k, :n]
        sy2[h, :n] = acc
        wx3_in[h, x] = acc[n - 8 :]
        one = {}
        if n > 8:
            one = send_all(
                FAR_X, x_peer, lambda xt: sy2.at[h, rows8(xt * 8, 8), :], lambda k: wx2_in.at[h, k - 1], s_x2.at[h], r_x2.at[h]
            )
        two = send_all(
            FAR_X, x_peer, lambda xt: sy2.at[h, pl.ds(n - 8, 8), :], lambda k: wx3_in.at[h, x], s_x3.at[h], r_x3.at[h]
        )
        return one, two

    def w1_y(h, got):
        arrive(got)
        n, m = FIRST[h], SMALL[h]
        acc = sx1[h, rows8(y * m, m), :]
        for k in range(NY - 1):
            acc = acc + wy1_in[h, k, :m]
        own = wf.at[h, rows8(x * n + y * m, m), :]
        own[...] = acc
        return send_all(FAR, y_peer, lambda yt: own, lambda k: own, s_y1g.at[h], r_y1g.at[h])

    def w2_x(h, got):
        arrive(got[0])
        arrive(got[1])
        n = SECOND[h]
        wf[h, rows8(CUT[h] + y * n + n - 8, 8), :] = (wx3_in[h, 0] + wx3_in[h, 1]) + (wx3_in[h, 2] + wx3_in[h, 3])
        if n == 8:
            return {}
        own = wf.at[h, rows8(CUT[h] + y * n + x * 8, 8), :]
        own[...] = (sy2[h, rows8(x * 8, 8), :] + wx2_in[h, 0]) + (wx2_in[h, 1] + wx2_in[h, 2])
        return send_all(FAR_X, x_peer, lambda xt: own, lambda k: own, s_x2g.at[h], r_x2g.at[h])

    def w2_x_gather(h, got):
        arrive(got)
        own = wf.at[h, rows8(CUT[h] + y * SECOND[h], SECOND[h]), :]
        return send_all(FAR, y_peer, lambda yt: own, lambda k: own, s_y2g.at[h], r_y2g.at[h])

    def w1_y_gather(h, got):
        arrive(got)
        own = wf.at[h, rows8(x * FIRST[h], FIRST[h]), :]
        return send_all(FAR_X, x_peer, lambda xt: own, lambda k: own, s_x1g.at[h], r_x1g.at[h])

    def factor(lo, hi):
        def body(k, carry):
            factor_panel(k, a)
            return carry
        lax.fori_loop(lo, hi, body, 0)

    with jax.named_scope("first_half"):
        gather_core(power.at[0], c_zg[0], f_zg[0], s_cg.at[0], r_cg.at[0])
        for c in f_zg[0]:
            c.wait_recv()
        x1_0 = w_first(0)
        w_second_dot(0)
        y2_0 = w_second(0)
        gather_core(power.at[1], c_zg[1], f_zg[1], s_cg.at[1], r_cg.at[1])
        for c in f_zg[1]:
            c.wait_recv()

    with jax.named_scope("gram_dot"):
        whole = jnp.concatenate([power[0], power[1]], axis=1)
        gram[...] = dot(whole, whole, ((0,), (0,)))
        gx[x] = gram[mine16, :]
        c_gx = send_all(FAR_X, x_peer, lambda xt: gx.at[x], lambda k: gx.at[x], s_gx, r_gx)

    with jax.named_scope("second_half"):
        x1_1 = w_first(1)
        w_second_dot(1)
        y1_0 = w1_x(0, x1_0)

    with jax.named_scope("gram_x"):
        arrive(c_gx)
        gy[y] = (gx[0] + gx[1]) + (gx[2] + gx[3])
        c_gy = send_all(FAR, y_peer, lambda yt: gy.at[y], lambda k: gy.at[y], s_gy, r_gy)

    with jax.named_scope("w_sums"):
        y2_1 = w_second(1)
        x2_0 = w2_y(0, y2_0)
        y1_1 = w1_x(1, x1_1)

    with jax.named_scope("gram_y"):
        arrive(c_gy)
        gram_all[mine16, :] = ((gy[0] + gy[1]) + (gy[2] + gy[3])) + ((gy[4] + gy[5]) + (gy[6] + gy[7]))
        c_gz, fs = gather_z(gram_all, s_gz, r_gz, s_gc, r_gc)

    with jax.named_scope("w_gathers"):
        y1g_0 = w1_y(0, y1_0)
        x2g_0 = w2_x(0, x2_0)
        x2_1 = w2_y(1, y2_1)
        y1g_1 = w1_y(1, y1_1)
        y2g_1 = w2_x_gather(1, w2_x(1, x2_1))

    with jax.named_scope("gram_z"):
        gather_core(gram_all, c_gz, fs, s_gc, r_gc)
        y2g_0 = w2_x_gather(0, x2g_0)
        for c in fs:
            c.wait_recv()
        a[:, :R] = gram_all[...]

    with jax.named_scope("factor_first"):
        x1g_0 = w1_y_gather(0, y1g_0)
        factor(0, 1)
    with jax.named_scope("w_last_gathers"):
        x1g_1 = w1_y_gather(1, y1g_1)
    with jax.named_scope("factor_rest"):
        factor(1, R // PANEL - 1)
        factor_panel(jnp.int32(R // PANEL - 1), a, last=True)

    with jax.named_scope("right"):
        arrive(x1g_0)
        arrive(x1g_1)
        right_ref[: CUT[0]] = dot3(jnp.concatenate([wf[0, : CUT[0]], wf[1, : CUT[0]]], axis=1), a[:, R:], ((1,), (1,)))
        arrive(y2g_0)
        arrive(y2g_1)
        right_ref[CUT[0] :] = dot3(jnp.concatenate([wf[0, CUT[0] :], wf[1, CUT[0] :]], axis=1), a[:, R:], ((1,), (1,)))
    with jax.named_scope("squares"):
        rt = right_ref[...]
        sums = jnp.sum((rt * rt).reshape(COLS // 8, 8, R), axis=0)
        sq[col] = jnp.sum(sums, axis=0, keepdims=True)
        cs = [
            send(sq.at[col], sq.at[col], s_sq.at[k - 1], r_sq.at[k - 1], col_peer(k))
            for k in (8, 7, 9, 6, 10, 5, 11, 4, 12, 3, 13, 2, 14, 1, 15)
        ]

    with jax.named_scope("ortho"):
        ortho_ref[...] = dot3(jnp.concatenate([power[0], power[1]], axis=1), a[:, R:], ((1,), (1,)))
    with jax.named_scope("momentum"):
        nm_ref[...] = buf[...] - (1.0 - KEEP_RATE) * dot3(right_ref[...], ortho_ref[...], ((1,), (1,)))

    with jax.named_scope("norms"):
        for c in cs:
            c.wait_recv()
        squares = sq[0]
        for k in range(1, 2 * NZ):
            squares = squares + sq[k]
        norms_ref[...] = jnp.broadcast_to(jnp.sqrt(squares) + NORM_EPS, (8, R))

    with jax.named_scope("wait_sent"):
        for c in sent:
            c.wait_send()


def finish(kept, nm_out, nb_out, up_out, nb, up, sems):
    nm, right, ortho, norms = (kept.at[pl.ds(at, n), :] for at, n in KEPT)

    def copy(i, src, dst):
        c = pltpu.make_async_copy(src, dst, sems.at[i])
        c.start()
        return c

    out = [copy(0, nm, nm_out)]
    nb[...] = right[...] / norms[:1]
    out.append(copy(1, nb, nb_out))
    up[...] = (math.sqrt(M * N / R) * dot3(nb[...], ortho[...], ((1,), (1,)))).astype(BF16)
    out.append(copy(2, up, up_out))
    for c in out:
        c.wait()


def shards(momentum, gradient, basis):
    hbm = pl.BlockSpec(memory_space=pltpu.HBM)
    v = lambda *s: pltpu.VMEM(s, F32)
    d = pltpu.SemaphoreType.DMA
    sems = []
    for n in (2, (2, 7), (2, 7), (2, 8), 3, 7, 7, 8, (2, 3), (2, 7), (2, 7), (2, 3), (2, 3), (2, 7), (2, 3), (2, 3), (2, 7), 15):
        sems += [d(n if isinstance(n, tuple) else (n,))] * 2
    out = jax.ShapeDtypeStruct
    vmem = pl.BlockSpec(memory_space=pltpu.VMEM)
    kept = pl.pallas_call(
        kernel,
        out_shape=out((2 * COLS + ROWS + 8, R), F32),
        in_specs=[hbm] * 3,
        out_specs=vmem,
        scratch_shapes=[
            v(COLS, ROWS), pltpu.VMEM((COLS, ROWS), BF16), v(COLS, R),
            v(COLS, ROWS), v(2, ROWS, 128), v(2, 128, 128), v(2, 128, 128), v(2, 7, 16, 128), v(2, ROWS, 128),
            v(R, R), v(NX, 16, R), v(NY, 16, R), v(R, R),
            v(2, COLS, 128), v(2, 3, FIRST[1], 128), v(2, FIRST[1], 128), v(2, 7, SMALL[1], 128),
            v(2, 7, SECOND[0], 128), v(2, SECOND[0], 128), v(2, 3, 8, 128), v(2, NX, 8, 128), v(2, COLS, 128),
            v(R, 2 * R), v(2 * NZ, 1, R),
            *sems, d((3, 2)),
        ],
        compiler_params=pltpu.CompilerParams(
            collective_id=0, has_side_effects=True, vmem_limit_bytes=40 << 20
        ),
    )(*(pltpu.with_memory_space_constraint(v, pltpu.HBM) for v in (momentum.T, gradient.T, basis)))
    nm, nb, up = pl.pallas_call(
        finish,
        out_shape=(out((COLS, ROWS), F32), out((COLS, R), F32), out((COLS, ROWS), BF16)),
        in_specs=[vmem],
        out_specs=(hbm,) * 3,
        scratch_shapes=[v(COLS, R), pltpu.VMEM((COLS, ROWS), BF16), d((3,))],
        compiler_params=pltpu.CompilerParams(vmem_limit_bytes=40 << 20),
    )(kept)
    return nm.T, nb, up.T


def solution(mesh):
    return jax.shard_map(
        shards,
        mesh=mesh,
        in_specs=(P("row", "col"), P("row", "col"), P("col", None)),
        out_specs=(P("row", "col"), P("col", None), P("row", "col")),
        check_vma=False,
    )
```

```python
import functools
import math

import jax
import jax.numpy as jnp
from jax import lax
from jax.experimental import pallas as pl
from jax.experimental.pallas import tpu as pltpu
from jax.sharding import PartitionSpec as P

M = 8192
N = 13312
R = 256
KEEP_RATE = 0.95
NORM_EPS = 1e-06

NX, NY, NZ = 4, 8, 8
ROWS = M // (NX * NY)
COLS = N // (2 * NZ)
CUT = (512, 768)
FIRST = tuple(n // NX for n in CUT)
SMALL = tuple(n // NY for n in FIRST)
SECOND = tuple((COLS - n) // NY for n in CUT)
PANEL = 32
KEPT = ((0, COLS), (COLS, COLS), (2 * COLS, ROWS), (2 * COLS + ROWS, 8))
FAR = (4, 3, 5, 2, 6, 1, 7)
NEAR = (1, 7, 2, 6, 3, 5, 4)
FAR_X = (2, 1, 3)
HALVES = (0, 1)
F32 = jnp.float32
BF16 = jnp.bfloat16
MESH = pl.DeviceIdType.MESH


def dot(a, b, dims):
    return lax.dot_general(
        a, b, (dims, ((), ())), precision=lax.Precision.HIGHEST, preferred_element_type=F32
    )


def dot3(a, b, dims):
    ah = a.astype(BF16)
    bh = b.astype(BF16)
    al = (a - ah.astype(F32)).astype(BF16)
    bl = (b - bh.astype(F32)).astype(BF16)
    one = lambda p, q: lax.dot_general(p, q, (dims, ((), ())), preferred_element_type=F32)
    return one(ah, bh) + (one(ah, bl) + one(al, bh))


def factor_panel(k, a, last=False):
    off = pl.multiple_of(k * PANEL, PANEL)
    base = pl.multiple_of(off // 128 * 128, 128)
    tiles = PANEL // 8
    sub = lax.broadcasted_iota(jnp.int32, (8, 128), 0)
    t = []
    for i in range(tiles):
        r = pl.ds(pl.multiple_of(off + 8 * i, 8), 8)
        row = a[r, :]
        own = pltpu.roll(a[r, pl.ds(base, 128)], lax.rem(128 - (off - base), 128), 1)
        t.append([own] + [row[:, 128 * q : 128 * q + 128] for q in range(4)])
    for b in range(tiles):
        cols = {}
        for i in range(b, tiles):
            for j in range(8):
                cols[i, j] = jnp.broadcast_to(t[i][0][:, 8 * b + j : 8 * b + j + 1], (8, 128))
        s = {}
        for j in range(8):
            for i in range(j, 8):
                s[i, j] = jnp.broadcast_to(cols[b, j][i : i + 1, :], (8, 128))
        scale = None
        for j in range(8):
            d = lax.rsqrt(s[j, j])
            l = {i: s[i, j] * d for i in range(j + 1, 8)}
            for m in range(j + 1, 8):
                for i in range(m, 8):
                    s[i, m] = s[i, m] - l[i] * l[m]
            pivot = [jnp.broadcast_to(t[b][q][j : j + 1, :], (8, 128)) * d for q in range(5)]
            for i in range(b, tiles):
                cols[i, j] = cols[i, j] * d
                for m in range(j + 1, 8):
                    cols[i, m] = cols[i, m] - cols[i, j] * l[m]
                times = cols[i, j] if i > b else jnp.where(sub > j, cols[i, j], 0.0)
                for q in range(5):
                    t[i][q] = t[i][q] - times * pivot[q]
            scale = d if j == 0 else jnp.where(sub == j, d, scale)
        for q in range(1, 5):
            t[b][q] = t[b][q] * scale
    r = jnp.concatenate([jnp.concatenate(t[i][1:], axis=1) for i in range(tiles)], axis=0)
    a[pl.ds(off, PANEL), R:] = r[:, R:]
    if last:
        return
    hi = r.astype(BF16).astype(F32)
    mi = (r - hi).astype(BF16).astype(F32)
    lo = r - hi - mi
    below = lax.broadcasted_iota(jnp.int32, (PANEL, R), 1) >= off + PANEL
    hl, ml, ll = (jnp.where(below, v[:, :R], 0.0).astype(BF16) for v in (hi, mi, lo))
    hr, mr, lr = hi.astype(BF16), mi.astype(BF16), lo.astype(BF16)
    lhs = jnp.concatenate([hl, hl, ml, ml, hl, ll], axis=0)
    rhs = jnp.concatenate([hr, mr, hr, mr, lr, hr], axis=0)
    a[...] = a[...] - lax.dot_general(
        lhs, rhs, (((0,), (0,)), ((), ())), preferred_element_type=F32
    )


def kernel(
    mom_hbm, grad_hbm, basis_hbm,
    out_ref,
    mom_ref, grad_ref, basis_ref, buf, part, core_in, half, z_in, power,
    gram, gx, gy, gram_all,
    wt, wx1_in, sx1, wy1_in, wy2_in, sy2, wx2_in, wx3_in, wf,
    a, sq,
    s_core, r_core, s_zr, r_zr, s_zg, r_zg, s_cg, r_cg,
    s_gx, r_gx, s_gy, r_gy, s_gz, r_gz, s_gc, r_gc,
    s_x1, r_x1, s_y1, r_y1, s_y2, r_y2, s_x2, r_x2, s_x3, r_x3,
    s_y1g, r_y1g, s_x1g, r_x1g, s_x2g, r_x2g, s_y2g, r_y2g,
    s_sq, r_sq, s_in,
):
    nm_ref, right_ref, ortho_ref, norms_ref = (out_ref.at[pl.ds(at, n), :] for at, n in KEPT)
    loads = [
        [
            pltpu.make_async_copy(src.at[pl.ds(at, COLS // 2), :], dst.at[pl.ds(at, COLS // 2), :], s_in.at[i, q])
            for i, (src, dst) in enumerate(((mom_hbm, mom_ref), (grad_hbm, grad_ref), (basis_hbm, basis_ref)))
        ]
        for q, at in enumerate((0, COLS // 2))
    ]
    for load in loads[0] + loads[1]:
        load.start()
    row = lax.axis_index("row")
    col = lax.axis_index("col")
    x, y = row // NY, lax.rem(row, NY)
    z, core = col // 2, lax.rem(col, 2)

    def x_peer(k):
        xt = lax.rem(x + k, NX)
        return xt, (xt * NY + y, col)

    def y_peer(k):
        yt = lax.rem(y + k, NY)
        return yt, (x * NY + yt, col)

    def z_peer(k):
        zt = lax.rem(z + k, NZ)
        return zt, (row, zt * 2 + core)

    sibling = (row, z * 2 + 1 - core)

    def col_peer(k):
        return (row, lax.rem(col + k, 2 * NZ))

    sent = []

    def send(src, dst, ssem, rsem, dev):
        copy = pltpu.make_async_remote_copy(
            src_ref=src, dst_ref=dst, send_sem=ssem, recv_sem=rsem,
            device_id=dev, device_id_type=MESH,
        )
        copy.start()
        sent.append(copy)
        return copy

    def rows8(start, n):
        return pl.ds(pl.multiple_of(start, 8), n)

    barrier = pltpu.get_barrier_semaphore()
    peers = [x_peer(k)[1] for k in range(1, NX)]
    peers += [y_peer(k)[1] for k in range(1, NY)]
    peers += [col_peer(k) for k in range(1, 2 * NZ)]
    for dev in peers:
        pl.semaphore_signal(barrier, inc=1, device_id=dev, device_id_type=MESH)

    ii = lax.broadcasted_iota(jnp.int32, (R, R), 0)
    jj = lax.broadcasted_iota(jnp.int32, (R, R), 1)
    a[:, R:] = jnp.where(ii == jj, 1.0, 0.0).astype(F32)

    mine128 = rows8(core * 128, 128)
    theirs128 = rows8((1 - core) * 128, 128)
    mine16 = rows8(core * 128 + z * 16, 16)

    def part_power(half_core, q):
        lanes = pl.ds(pl.multiple_of(half_core * 128, 128), 128)
        some = pl.ds(q * (COLS // 2), COLS // 2)
        return dot(buf[some, lanes], basis_ref[some, :], ((0,), (0,)))

    def send_all(order, peer, src, dst, ss, rr):
        out = {}
        for k in order:
            at, dev = peer(k)
            out[k] = send(src(at), dst(k), ss.at[k - 1], rr.at[k - 1], dev)
        return out

    def arrive(copies):
        for c in copies.values():
            c.wait_recv()

    with jax.named_scope("partial_power"):
        theirs, mine = [], []
        for q in range(2):
            for load in loads[q]:
                load.wait()
            some = pl.ds(q * (COLS // 2), COLS // 2)
            buf[some, :] = mom_ref[some, :] + grad_ref[some, :].astype(F32)
            theirs.append(part_power(1 - core, q))
            if q == 0:
                mine.append(part_power(core, q))
        theirs = theirs[0] + theirs[1]
        for h in HALVES:
            part[h, theirs128, :] = theirs[:, 128 * h : 128 * h + 128]
        pl.semaphore_wait(barrier, len(peers))
        c_core = [send(part.at[h, theirs128, :], core_in.at[h], s_core.at[h], r_core.at[h], sibling) for h in HALVES]
        mine = mine[0] + part_power(core, 1)

    c_z = [None, None]
    with jax.named_scope("power_core"):
        for h in HALVES:
            c_core[h].wait_recv()
            half[h] = mine[:, 128 * h : 128 * h + 128] + core_in[h]
            c_z[h] = send_all(
                FAR, z_peer, lambda zt: half.at[h, rows8(zt * 16, 16), :], lambda k: z_in.at[h, k - 1], s_zr.at[h], r_zr.at[h]
            )

    def gather_z(ref, ss, rr, sc, rc):
        own = ref.at[mine16, :]
        cs = send_all(FAR, z_peer, lambda zt: own, lambda k: own, ss, rr)
        return cs, [send(own, own, sc.at[0], rc.at[0], sibling)]

    def gather_core(ref, cs, fs, sc, rc):
        for k in NEAR:
            cs[k].wait_recv()
            zs = lax.rem(z + NZ - k, NZ)
            other = ref.at[rows8(core * 128 + zs * 16, 16), :]
            fs.append(send(other, other, sc.at[k], rc.at[k], sibling))

    c_zg, f_zg = [None, None], [None, None]
    with jax.named_scope("power_z"):
        for h in HALVES:
            total = half[h, rows8(z * 16, 16), :]
            for k in NEAR:
                c_z[h][k].wait_recv()
                total = total + z_in[h, k - 1]
            power[h, mine16, :] = total
            c_zg[h], f_zg[h] = gather_z(power.at[h], s_zg.at[h], r_zg.at[h], s_cg.at[h], r_cg.at[h])

    def w_first(h):
        wt[h, : CUT[h]] = dot(buf[: CUT[h]], power[h], ((1,), (0,)))
        n = FIRST[h]
        return send_all(
            FAR_X, x_peer, lambda xt: wt.at[h, rows8(xt * n, n), :], lambda k: wx1_in.at[h, k - 1, pl.ds(0, n), :],
            s_x1.at[h], r_x1.at[h],
        )

    def w_second_dot(h):
        wt[h, CUT[h] :] = dot(buf[CUT[h] :], power[h], ((1,), (0,)))

    def w_second(h):
        n = SECOND[h]
        return send_all(
            FAR, y_peer, lambda yt: wt.at[h, rows8(CUT[h] + yt * n, n), :], lambda k: wy2_in.at[h, k - 1, pl.ds(0, n), :],
            s_y2.at[h], r_y2.at[h],
        )

    def w1_x(h, got):
        arrive(got)
        n, m = FIRST[h], SMALL[h]
        sx1[h, :n] = (wt[h, rows8(x * n, n), :] + wx1_in[h, 0, :n]) + (wx1_in[h, 1, :n] + wx1_in[h, 2, :n])
        return send_all(
            FAR, y_peer, lambda yt: sx1.at[h, rows8(yt * m, m), :], lambda k: wy1_in.at[h, k - 1, pl.ds(0, m), :],
            s_y1.at[h], r_y1.at[h],
        )

    def w2_y(h, got):
        arrive(got)
        n = SECOND[h]
        acc = wt[h, rows8(CUT[h] + y * n, n), :]
        for k in range(NY - 1):
            acc = acc + wy2_in[h, k, :n]
        sy2[h, :n] = acc
        wx3_in[h, x] = acc[n - 8 :]
        one = {}
        if n > 8:
            one = send_all(
                FAR_X, x_peer, lambda xt: sy2.at[h, rows8(xt * 8, 8), :], lambda k: wx2_in.at[h, k - 1], s_x2.at[h], r_x2.at[h]
            )
        two = send_all(
            FAR_X, x_peer, lambda xt: sy2.at[h, pl.ds(n - 8, 8), :], lambda k: wx3_in.at[h, x], s_x3.at[h], r_x3.at[h]
        )
        return one, two

    def w1_y(h, got):
        arrive(got)
        n, m = FIRST[h], SMALL[h]
        acc = sx1[h, rows8(y * m, m), :]
        for k in range(NY - 1):
            acc = acc + wy1_in[h, k, :m]
        own = wf.at[h, rows8(x * n + y * m, m), :]
        own[...] = acc
        return send_all(FAR, y_peer, lambda yt: own, lambda k: own, s_y1g.at[h], r_y1g.at[h])

    def w2_x(h, got):
        arrive(got[0])
        arrive(got[1])
        n = SECOND[h]
        wf[h, rows8(CUT[h] + y * n + n - 8, 8), :] = (wx3_in[h, 0] + wx3_in[h, 1]) + (wx3_in[h, 2] + wx3_in[h, 3])
        if n == 8:
            return {}
        own = wf.at[h, rows8(CUT[h] + y * n + x * 8, 8), :]
        own[...] = (sy2[h, rows8(x * 8, 8), :] + wx2_in[h, 0]) + (wx2_in[h, 1] + wx2_in[h, 2])
        return send_all(FAR_X, x_peer, lambda xt: own, lambda k: own, s_x2g.at[h], r_x2g.at[h])

    def w2_x_gather(h, got):
        arrive(got)
        own = wf.at[h, rows8(CUT[h] + y * SECOND[h], SECOND[h]), :]
        return send_all(FAR, y_peer, lambda yt: own, lambda k: own, s_y2g.at[h], r_y2g.at[h])

    def w1_y_gather(h, got):
        arrive(got)
        own = wf.at[h, rows8(x * FIRST[h], FIRST[h]), :]
        return send_all(FAR_X, x_peer, lambda xt: own, lambda k: own, s_x1g.at[h], r_x1g.at[h])

    def factor(lo, hi):
        def body(k, carry):
            factor_panel(k, a)
            return carry
        lax.fori_loop(lo, hi, body, 0)

    with jax.named_scope("first_half"):
        gather_core(power.at[0], c_zg[0], f_zg[0], s_cg.at[0], r_cg.at[0])
        for c in f_zg[0]:
            c.wait_recv()
        x1_0 = w_first(0)
        w_second_dot(0)
        y2_0 = w_second(0)
        gather_core(power.at[1], c_zg[1], f_zg[1], s_cg.at[1], r_cg.at[1])
        for c in f_zg[1]:
            c.wait_recv()

    with jax.named_scope("gram_dot"):
        whole = jnp.concatenate([power[0], power[1]], axis=1)
        gram[...] = dot(power[core], whole, ((0,), (0,)))
        gx[x] = gram[rows8(z * 16, 16), :]
        c_gx = send_all(FAR_X, x_peer, lambda xt: gx.at[x], lambda k: gx.at[x], s_gx, r_gx)

    with jax.named_scope("second_half"):
        x1_1 = w_first(1)
        w_second_dot(1)
        y1_0 = w1_x(0, x1_0)

    with jax.named_scope("gram_x"):
        arrive(c_gx)
        gy[y] = (gx[0] + gx[1]) + (gx[2] + gx[3])
        c_gy = send_all(FAR, y_peer, lambda yt: gy.at[y], lambda k: gy.at[y], s_gy, r_gy)

    with jax.named_scope("w_sums"):
        y2_1 = w_second(1)
        x2_0 = w2_y(0, y2_0)
        y1_1 = w1_x(1, x1_1)

    with jax.named_scope("gram_y"):
        arrive(c_gy)
        gram_all[mine16, :] = ((gy[0] + gy[1]) + (gy[2] + gy[3])) + ((gy[4] + gy[5]) + (gy[6] + gy[7]))
        c_gz, fs = gather_z(gram_all, s_gz, r_gz, s_gc, r_gc)

    with jax.named_scope("w_gathers"):
        y1g_0 = w1_y(0, y1_0)
        x2g_0 = w2_x(0, x2_0)
        x2_1 = w2_y(1, y2_1)
        y1g_1 = w1_y(1, y1_1)
        y2g_1 = w2_x_gather(1, w2_x(1, x2_1))

    with jax.named_scope("gram_z"):
        gather_core(gram_all, c_gz, fs, s_gc, r_gc)
        y2g_0 = w2_x_gather(0, x2g_0)
        for c in fs:
            c.wait_recv()
        a[:, :R] = gram_all[...]

    with jax.named_scope("factor_first"):
        x1g_0 = w1_y_gather(0, y1g_0)
        factor(0, 1)
    with jax.named_scope("w_last_gathers"):
        x1g_1 = w1_y_gather(1, y1g_1)
    with jax.named_scope("factor_rest"):
        factor(1, R // PANEL - 1)
        factor_panel(jnp.int32(R // PANEL - 1), a, last=True)

    with jax.named_scope("right"):
        arrive(x1g_0)
        arrive(x1g_1)
        right_ref[: CUT[0]] = dot3(jnp.concatenate([wf[0, : CUT[0]], wf[1, : CUT[0]]], axis=1), a[:, R:], ((1,), (1,)))
        arrive(y2g_0)
        arrive(y2g_1)
        right_ref[CUT[0] :] = dot3(jnp.concatenate([wf[0, CUT[0] :], wf[1, CUT[0] :]], axis=1), a[:, R:], ((1,), (1,)))
    with jax.named_scope("squares"):
        rt = right_ref[...]
        sums = jnp.sum((rt * rt).reshape(COLS // 8, 8, R), axis=0)
        sq[col] = jnp.sum(sums, axis=0, keepdims=True)
        cs = [
            send(sq.at[col], sq.at[col], s_sq.at[k - 1], r_sq.at[k - 1], col_peer(k))
            for k in (8, 7, 9, 6, 10, 5, 11, 4, 12, 3, 13, 2, 14, 1, 15)
        ]

    with jax.named_scope("ortho"):
        ortho_ref[...] = dot3(jnp.concatenate([power[0], power[1]], axis=1), a[:, R:], ((1,), (1,)))
    with jax.named_scope("momentum"):
        nm_ref[...] = buf[...] - (1.0 - KEEP_RATE) * dot3(right_ref[...], ortho_ref[...], ((1,), (1,)))

    with jax.named_scope("norms"):
        for c in cs:
            c.wait_recv()
        squares = sq[0]
        for k in range(1, 2 * NZ):
            squares = squares + sq[k]
        norms_ref[...] = jnp.broadcast_to(jnp.sqrt(squares) + NORM_EPS, (8, R))

    with jax.named_scope("wait_sent"):
        for c in sent:
            c.wait_send()


def finish(kept, nm_out, nb_out, up_out, nb, up, sems):
    nm, right, ortho, norms = (kept.at[pl.ds(at, n), :] for at, n in KEPT)

    def copy(i, src, dst):
        c = pltpu.make_async_copy(src, dst, sems.at[i])
        c.start()
        return c

    out = [copy(0, nm, nm_out)]
    nb[...] = right[...] / norms[:1]
    out.append(copy(1, nb, nb_out))
    up[...] = (math.sqrt(M * N / R) * dot3(nb[...], ortho[...], ((1,), (1,)))).astype(BF16)
    out.append(copy(2, up, up_out))
    for c in out:
        c.wait()


def shards(momentum, gradient, basis):
    hbm = pl.BlockSpec(memory_space=pltpu.HBM)
    v = lambda *s: pltpu.VMEM(s, F32)
    d = pltpu.SemaphoreType.DMA
    sems = []
    for n in (2, (2, 7), (2, 7), (2, 8), 3, 7, 7, 8, (2, 3), (2, 7), (2, 7), (2, 3), (2, 3), (2, 7), (2, 3), (2, 3), (2, 7), 15):
        sems += [d(n if isinstance(n, tuple) else (n,))] * 2
    out = jax.ShapeDtypeStruct
    vmem = pl.BlockSpec(memory_space=pltpu.VMEM)
    kept = pl.pallas_call(
        kernel,
        out_shape=out((2 * COLS + ROWS + 8, R), F32),
        in_specs=[hbm] * 3,
        out_specs=vmem,
        scratch_shapes=[
            v(COLS, ROWS), pltpu.VMEM((COLS, ROWS), BF16), v(COLS, R),
            v(COLS, ROWS), v(2, ROWS, 128), v(2, 128, 128), v(2, 128, 128), v(2, 7, 16, 128), v(2, ROWS, 128),
            v(128, R), v(NX, 16, R), v(NY, 16, R), v(R, R),
            v(2, COLS, 128), v(2, 3, FIRST[1], 128), v(2, FIRST[1], 128), v(2, 7, SMALL[1], 128),
            v(2, 7, SECOND[0], 128), v(2, SECOND[0], 128), v(2, 3, 8, 128), v(2, NX, 8, 128), v(2, COLS, 128),
            v(R, 2 * R), v(2 * NZ, 1, R),
            *sems, d((3, 2)),
        ],
        compiler_params=pltpu.CompilerParams(
            collective_id=0, has_side_effects=True, vmem_limit_bytes=40 << 20
        ),
    )(*(pltpu.with_memory_space_constraint(v, pltpu.HBM) for v in (momentum.T, gradient.T, basis)))
    nm, nb, up = pl.pallas_call(
        finish,
        out_shape=(out((COLS, ROWS), F32), out((COLS, R), F32), out((COLS, ROWS), BF16)),
        in_specs=[vmem],
        out_specs=(hbm,) * 3,
        scratch_shapes=[v(COLS, R), pltpu.VMEM((COLS, ROWS), BF16), d((3,))],
        compiler_params=pltpu.CompilerParams(vmem_limit_bytes=40 << 20),
    )(kept)
    return nm.T, nb, up.T


def solution(mesh):
    return jax.shard_map(
        shards,
        mesh=mesh,
        in_specs=(P("row", "col"), P("row", "col"), P("col", None)),
        out_specs=(P("row", "col"), P("col", None), P("row", "col")),
        check_vma=False,
    )
```
